512 devices in a mesh: tm: 64 (over y, x, core), space: 8 (over z).
Axes of the slice: x: 4, y: 8, z: 8, core: 2. Of those that a mesh axis runs over, the one named last changes fastest.
Arguments:
- states: float32 [64, 21, 8192], P('tm', None, 'space'), may hold values from -6 to 6
- neighbour: int32 [3, 8192], P(None, 'space'), may hold values from -64 to 64, as said below
- edge_x: float32 [3, 8192], P(None, 'space'), may hold values from -0.3 to 0.3
- edge_y: float32 [3, 8192], P(None, 'space'), may hold values from -0.3 to 0.3
- edge_damp: float32 [3, 8192], P(None, 'space'), may hold values from 0.03 to 0.15
- coriolis: float32 [8192], P('space'), may hold values from -0.2 to 0.2
- flux_x: float32 [21, 21], replicated, may hold values from -0.625 to 0.625
- flux_y: float32 [21, 21], replicated, may hold values from -0.625 to 0.625
- rotation: float32 [21, 21], replicated, may hold values from -1.25 to 1.25
- restrict_matrix: float32 [4, 21], replicated, may hold values from -2.5 to 2.5
- prolong_matrix: float32 [21, 4], replicated, may hold values from -6 to 6
- restrict_index: int32 [8192], P('space'), may hold values from 0 to 31, as said below
- coarse_inverse: float32 [4, 4, 256], replicated, may hold values from -1 to 1
Outputs:
- new_states: float32 [64, 21, 8192], P('tm', None, 'space')
The draws below stay inside these ranges and needn't reach their ends.
Inputs may be any that keep to these rules, and one draw needn't show every extreme that they name: Triangle c borders triangles (c + neighbour[e, c]) mod 8192 for e = 0, 1, 2. `restrict_index`: every coarse triangle of every partition holds at least one triangle.
All inputs are finite; a program needn't handle non-finite values.
Results may differ from the reference program's by a relative error of at most 0.0003.
Values sent between devices are 32-bit elements; how exact they have to be, the bound alone decides.
No kernel may reach another device: no remote copies, remote signals or barrier semaphores. Data moves between devices by JAX's collectives and lax.ppermute only.
A program may use at most 64 MiB of HBM per device.

```python
import math
import jax
import jax.numpy as jnp
from jax import lax

DOF = 21
CDOF = 4
CELLS_DEV = 1024
FINE_PER_COARSE = 32
HW = 64
STEPS = 16
COARSE_STEPS = 4
SLICES = 64
CELLS = 8192
COARSE_DEV = 32
NCOARSE = 256
N_SPACE = 8


def draw_neighbour(key, part):
    key = jax.random.fold_in(key, 11)
    spread_key, spot_key = jax.random.split(key)
    offsets = jax.random.randint(spread_key, (3, CELLS), -HW, HW + 1)
    spots = jax.random.randint(spot_key, (2,), 0, CELLS)
    offsets = offsets.at[0, spots[0]].set(-HW)
    offsets = offsets.at[1, spots[1]].set(HW)
    return offsets.astype(jnp.int32)


def draw_restrict_index(key, part):
    key = jax.random.fold_in(key, 23)
    cells = jnp.arange(CELLS, dtype=jnp.int32) % CELLS_DEV
    blocks = cells // FINE_PER_COARSE
    inner = cells % FINE_PER_COARSE
    moves = jax.random.randint(key, (CELLS,), 0, 2)
    lower = jnp.where(inner == 0, moves, 0)
    upper = jnp.where(inner == FINE_PER_COARSE - 1, moves, 0)
    return jnp.clip(blocks - lower + upper, 0, COARSE_DEV - 1).astype(jnp.int32)


def draw_coarse_inverse(key, part):
    key = jax.random.fold_in(key, 37)
    keys = jax.random.split(key, 6)
    turn_a = jax.random.uniform(keys[0], (NCOARSE,), jnp.float32, -math.pi, math.pi)
    turn_b = jax.random.uniform(keys[1], (NCOARSE,), jnp.float32, -math.pi, math.pi)
    turn_c = jax.random.uniform(keys[2], (NCOARSE,), jnp.float32, -math.pi, math.pi)
    lasting_share = 0.5
    groups = jax.random.uniform(keys[3], (NCOARSE // 16,), jnp.float32) < lasting_share
    lasting = jnp.repeat(groups, 16)
    retained = jnp.exp(jax.random.uniform(keys[4], (CDOF, NCOARSE), jnp.float32, math.log(0.15), math.log(0.6)))
    slow_rate = jnp.exp(jnp.log(retained) / (COARSE_STEPS * SLICES))
    memory = jax.random.uniform(keys[5], (CDOF, NCOARSE), jnp.float32, 30.0, 50.0)
    fast_rate = jnp.exp(math.log(0.1) / memory)
    decay = jnp.where(lasting[None, :], slow_rate, fast_rate)
    cos_a = jnp.cos(turn_a)
    sin_a = jnp.sin(turn_a)
    cos_b = jnp.cos(turn_b)
    sin_b = jnp.sin(turn_b)
    cos_c = jnp.cos(turn_c)
    sin_c = jnp.sin(turn_c)
    row_zero = jnp.stack([cos_b * cos_a, -(cos_b * sin_a), -(sin_b * cos_c), sin_b * sin_c])
    row_one = jnp.stack([cos_b * sin_a, cos_b * cos_a, -(sin_b * sin_c), -(sin_b * cos_c)])
    row_two = jnp.stack([sin_b * cos_a, -(sin_b * sin_a), cos_b * cos_c, -(cos_b * sin_c)])
    row_three = jnp.stack([sin_b * sin_a, sin_b * cos_a, cos_b * sin_c, cos_b * cos_c])
    blocks = jnp.stack([row_zero, row_one, row_two, row_three])
    return (decay[:, None, :] * blocks).astype(jnp.float32)


def shard_levels(own_key, shape, shards, low, top_value):
    loudness = 1.0
    for dim, shards_of in shards:
        heights = jax.random.uniform(jax.random.fold_in(jax.random.fold_in(own_key, 6), dim), (shards_of,), jnp.float32, low / len(shards), top_value / len(shards))
        loudness = loudness * jnp.repeat(jnp.exp(heights), shape[dim] // shards_of).reshape((-1,) + (1,) * (len(shape) - 1 - dim))
    return loudness


def scatter_about(own_key, shape, scale, most, cuts=(), held_as=jnp.bfloat16):
    values = scale * jax.random.normal(own_key, shape, jnp.float32)
    if cuts:
        values = values * shard_levels(own_key, shape, cuts, -0.22, 0.18)
    return jnp.clip(values, -most, most).astype(held_as)


def setup_inputs(seed: int = 0) -> dict:
    splits = jax.random.split(jax.random.key(seed), 14)
    states = scatter_about(splits[0], (SLICES, DOF, CELLS), 1.0, 6.0, ((0, 64), (2, 8)), jnp.float32)
    neighbour = draw_neighbour(jax.random.fold_in(splits[13], 71), 0)
    edge_x = scatter_about(splits[2], (3, CELLS), 0.05, 0.3, ((1, 8),), jnp.float32)
    edge_y = scatter_about(splits[3], (3, CELLS), 0.05, 0.3, ((1, 8),), jnp.float32)
    edge_damp = jnp.clip(jnp.exp(math.log(0.15) - 1.609438 * jax.random.uniform(splits[4], (3, CELLS), jnp.float32) ** shard_levels(splits[4], (3, CELLS), ((1, 8),), -0.2, 0.2)), 0.03, 0.15)
    coriolis = jnp.clip(jax.random.uniform(splits[5], (CELLS,), jnp.float32, -0.2, 0.2) * shard_levels(splits[5], (CELLS,), ((0, 8),), -0.4, 0.0), -0.2, 0.2)
    flux_x = scatter_about(splits[6], (DOF, DOF), (4 * DOF) ** -0.5, 0.625, (), jnp.float32)
    flux_y = scatter_about(splits[7], (DOF, DOF), (4 * DOF) ** -0.5, 0.625, (), jnp.float32)
    rotation = scatter_about(splits[8], (DOF, DOF), DOF ** -0.5, 1.25, (), jnp.float32)
    restrict_matrix = scatter_about(splits[9], (CDOF, DOF), (DOF // 4) ** -0.5, 2.5, (), jnp.float32)
    prolong_matrix = scatter_about(splits[10], (DOF, CDOF), 1 ** -0.5, 6.0, (), jnp.float32)
    restrict_index = draw_restrict_index(jax.random.fold_in(splits[13], 71), 0)
    coarse_inverse = draw_coarse_inverse(jax.random.fold_in(splits[13], 71), 0)
    return {"states": states, "neighbour": neighbour, "edge_x": edge_x, "edge_y": edge_y, "edge_damp": edge_damp, "coriolis": coriolis, "flux_x": flux_x, "flux_y": flux_y, "rotation": rotation, "restrict_matrix": restrict_matrix, "prolong_matrix": prolong_matrix, "restrict_index": restrict_index, "coarse_inverse": coarse_inverse}


coupling = 0.1
opposite = 0.25
highest = lax.Precision.HIGHEST


def periodic_pad(values):
    return jnp.concatenate([values[:, -HW:], values, values[:, :HW]], axis=1)


def tendency(source, offsets, edge_x, edge_y, edge_damp, coriolis, stencil):
    span_cells = offsets.shape[1]
    center = lax.slice_in_dim(source, HW, HW + span_cells, axis=1)
    places = HW + jnp.arange(span_cells, dtype=jnp.int32)
    along_x = jnp.zeros_like(center)
    along_y = jnp.zeros_like(center)
    damped = jnp.zeros_like(center)
    for edge_index in range(3):
        nearby = jnp.take(source, places + offsets[edge_index], axis=1)
        difference = nearby - center
        along_x = along_x + edge_x[edge_index] * difference
        along_y = along_y + edge_y[edge_index] * difference
        damped = damped + edge_damp[edge_index] * difference
    stacked = jnp.concatenate([along_x, along_y, coriolis * center], axis=0)
    return jnp.dot(stencil, stacked, precision=highest) + damped


def make_onehot(index):
    return (index[None, :] == jnp.arange(COARSE_DEV, dtype=jnp.int32)[:, None]).astype(jnp.float32)


def restrict(values, onehot, restrict_matrix):
    totals = jnp.einsum("dc,kc->dk", values, onehot, precision=highest)
    counts = jnp.sum(onehot, axis=1)
    return jnp.dot(restrict_matrix, totals, precision=highest) / counts


def prolong(correction, onehot, prolong_matrix):
    return jnp.dot(jnp.dot(prolong_matrix, correction, precision=highest), onehot, precision=highest)


def coarse_step(vector, inverse_blocks):
    half_cycle = vector.shape[1] // 2
    blended = vector + coupling * (jnp.roll(vector, 1, axis=1) + jnp.roll(vector, -1, axis=1) - 2.0 * vector)
    blended = blended + opposite * (jnp.roll(vector, half_cycle, axis=1) - vector)
    result = inverse_blocks[:, 0, :] * blended[0]
    for column in range(1, CDOF):
        result = result + inverse_blocks[:, column, :] * blended[column]
    return result


def coarse_slice(vector, inverse_blocks):
    for repeat in range(COARSE_STEPS):
        vector = coarse_step(vector, inverse_blocks)
    return vector


def reference(states, neighbour, edge_x, edge_y, edge_damp, coriolis, flux_x, flux_y, rotation, restrict_matrix, prolong_matrix, restrict_index, coarse_inverse):
    stencil = jnp.concatenate([flux_x, flux_y, rotation], axis=1)

    def propagate(values):
        def advance(index_step, current):
            first_rate = tendency(periodic_pad(current), neighbour, edge_x, edge_y, edge_damp, coriolis, stencil)
            middle = current + first_rate
            second_rate = tendency(periodic_pad(middle), neighbour, edge_x, edge_y, edge_damp, coriolis, stencil)
            return current + 0.5 * (first_rate + second_rate)
        return lax.fori_loop(0, STEPS, advance, values)

    finals = lax.map(propagate, states)
    index_parts = restrict_index.reshape(N_SPACE, CELLS_DEV)

    def restrict_all(values):
        parts = values.reshape(DOF, N_SPACE, CELLS_DEV).transpose(1, 0, 2)
        pieces = lax.map(lambda bundle: restrict(bundle[0], make_onehot(bundle[1]), restrict_matrix), (parts, index_parts))
        return pieces.transpose(1, 0, 2).reshape(CDOF, NCOARSE)

    starts = lax.map(restrict_all, states)
    ends = lax.map(restrict_all, finals)
    coarse_starts = lax.map(lambda vector: coarse_slice(vector, coarse_inverse), starts)
    jumps = ends - coarse_starts

    def link(previous, jump_now):
        linked = coarse_slice(previous, coarse_inverse) + jump_now
        return linked, linked

    finished, rest = lax.scan(link, ends[0], jumps[1:])
    chain = jnp.concatenate([ends[:1], rest], axis=0)
    corrections = chain - ends

    def correct_slice(bundle):
        fine_now, correction_now = bundle
        fine_parts = fine_now.reshape(DOF, N_SPACE, CELLS_DEV).transpose(1, 0, 2)
        coarse_parts = correction_now.reshape(CDOF, N_SPACE, COARSE_DEV).transpose(1, 0, 2)

        def correct_part(inner):
            return inner[0] + prolong(inner[1], make_onehot(inner[2]), prolong_matrix)

        fixed = lax.map(correct_part, (fine_parts, coarse_parts, index_parts))
        return fixed.transpose(1, 0, 2).reshape(DOF, CELLS)

    return lax.map(correct_slice, (finals, corrections))
```

```python
import functools

import jax
import jax.numpy as jnp
from jax import lax
from jax.experimental import pallas as pl
from jax.experimental.pallas import tpu as pltpu
from jax.sharding import PartitionSpec as P

DOF = 21
CDOF = 4
ROWS = 24
LANES = 128
HALF = 64
CELLS_DEV = 1024
COARSE_DEV = 32
COARSE_STEPS = 4
PARTS = 8
SLICES = 64
BLOCKS = CELLS_DEV // LANES
PHASE_STEPS = 8
SEGMENT = 2
WINDOW = 3 * BLOCKS

coupling = 0.1
opposite = 0.25
highest = lax.Precision.HIGHEST
f32 = jnp.float32
bf16 = jnp.bfloat16
vmem = pl.BlockSpec(memory_space=pltpu.VMEM)


def lane_gather(values, index):
    numbers = lax.GatherDimensionNumbers(
        offset_dims=(),
        collapsed_slice_dims=(1,),
        start_index_map=(1,),
        operand_batching_dims=(0,),
        start_indices_batching_dims=(0,),
    )
    return lax.gather(
        values, index[..., None], numbers, (1, 1), mode=lax.GatherScatterMode.PROMISE_IN_BOUNDS
    )


def two_terms(values):
    high = values.astype(bf16)
    return high, (values - high.astype(f32)).astype(bf16)


def lanes_of(block, count=1):
    return slice(block * LANES, (block + count) * LANES)


def fill_window(state_refs, mesh_refs, field, places, coefs):
    inside = lax.broadcasted_iota(jnp.int32, (ROWS, CELLS_DEV), 0) < DOF
    lane = lax.broadcasted_iota(jnp.int32, (8, CELLS_DEV), 1) % LANES
    edge = jnp.zeros((ROWS, LANES), f32)
    field[:, lanes_of(0)] = edge
    field[:, lanes_of(WINDOW + 1)] = edge
    for part, (state_ref, mesh_ref) in enumerate(zip(state_refs, mesh_refs)):
        cells = lanes_of(1 + part * BLOCKS, BLOCKS)
        field[:, cells] = jnp.where(inside, state_ref[0:ROWS, :], 0.0)
        for e in range(3):
            offset = mesh_ref[DOF + e : DOF + e + 1, :].astype(jnp.int32)
            target = jnp.broadcast_to(offset, (8, CELLS_DEV)) + lane
            within = (target >= 0) & (target < LANES)
            places[e, :, cells] = (target & (LANES - 1)) + jnp.where(within, 0, LANES)
        for row in range(10):
            coefs[row, :, cells] = jnp.broadcast_to(
                mesh_ref[DOF + 3 + row : DOF + 4 + row, :], (8, CELLS_DEV)
            )


def block_rate(source, block, places, coefs, stencil, low_half):
    here = lanes_of(block)
    centre = []
    around = []
    for r in range(3):
        rows = slice(8 * r, 8 * r + 8)
        centre.append(source[rows, here])
        around.append(
            jnp.where(low_half, source[rows, lanes_of(block + 1)], source[rows, lanes_of(block - 1)])
        )
    sums = [[None] * 3 for _ in range(3)]
    for e in range(3):
        place = places[e, :, here]
        index = place & (LANES - 1)
        within = place < LANES
        found = [lane_gather(piece, index) for piece in centre + around]
        for r in range(3):
            difference = jnp.where(within, found[r], found[3 + r]) - centre[r]
            for a in range(3):
                term = coefs[3 * a + e, :, here] * difference
                sums[a][r] = term if e == 0 else sums[a][r] + term
    turned = [coefs[9, :, here] * piece for piece in centre]
    stacked = jnp.concatenate(sums[0] + sums[1] + turned + [jnp.zeros((8, LANES), f32)], axis=0)
    high, low = two_terms(stacked)
    mixed = jnp.dot(
        stencil, jnp.concatenate([high, low, high], axis=0), preferred_element_type=f32
    )
    return mixed + jnp.concatenate(sums[2], axis=0)


def march(field, middle, places, coefs, stencil_ref):
    low_half = lax.broadcasted_iota(jnp.int32, (8, LANES), 1) < HALF
    edge = jnp.zeros((ROWS, LANES), f32)
    middle[:, lanes_of(0)] = edge
    middle[:, lanes_of(WINDOW + 1)] = edge

    for first in range(0, PHASE_STEPS, SEGMENT):
        blocks = range(1 + first, 1 + WINDOW - first)

        def step(index, carry):
            stencil = stencil_ref[...]
            for b in blocks:
                rate = block_rate(field, b, places, coefs, stencil, low_half)
                middle[:, lanes_of(b)] = field[:, lanes_of(b)] + rate
            for b in blocks:
                rate = block_rate(middle, b, places, coefs, stencil, low_half)
                here = lanes_of(b)
                field[:, here] = 0.5 * (field[:, here] + middle[:, here] + rate)
            return carry

        lax.fori_loop(0, SEGMENT, step, 0)


def first_phase_kernel(left, centre, right, stencil_ref, out, field, middle, places, coefs):
    packs = (left, centre, right)
    fill_window(packs, packs, field, places, coefs)
    march(field, middle, places, coefs, stencil_ref)
    out[...] = field[:, lanes_of(1 + BLOCKS, BLOCKS)]


def restricted(values, members, restrict_matrix):
    contract = (((1,), (1,)), ((), ()))
    first, rest = two_terms(values)
    second, third = two_terms(values - first.astype(f32))
    totals = jnp.zeros((ROWS, COARSE_DEV), f32)
    for term in (third, second, first):
        totals = totals + lax.dot_general(term, members, contract, preferred_element_type=f32)
    counts = lax.dot_general(
        jnp.ones((16, CELLS_DEV), bf16), members, contract, preferred_element_type=f32
    )[0:1]
    result = jnp.zeros((CDOF, COARSE_DEV), f32)
    for d in range(DOF):
        result = result + restrict_matrix[:, d : d + 1] * totals[d : d + 1, :]
    return result / counts


def in_one_row(coarse):
    return jnp.concatenate([coarse[i : i + 1, :] for i in range(CDOF)], axis=1)


def second_phase_kernel(
    left, centre, right, left_mesh, centre_mesh, right_mesh, stencil_ref, index_ref, matrix_ref,
    out, message, field, middle, places, coefs,
):
    fill_window(
        (left, centre, right), (left_mesh, centre_mesh, right_mesh), field, places, coefs
    )
    march(field, middle, places, coefs, stencil_ref)
    fine = field[:, lanes_of(1 + BLOCKS, BLOCKS)]
    out[...] = fine
    members = (
        lax.broadcasted_iota(jnp.int32, (COARSE_DEV, CELLS_DEV), 0) == index_ref[...]
    ).astype(f32).astype(bf16)
    matrix = matrix_ref[...]
    inside = lax.broadcasted_iota(jnp.int32, (ROWS, CELLS_DEV), 0) < DOF
    start = jnp.where(inside, centre_mesh[0:ROWS, :], 0.0)
    message[0:1, :] = in_one_row(restricted(fine, members, matrix))
    message[1:2, :] = in_one_row(restricted(start, members, matrix))


def coarse_step(vector, blocks, first_lane, last_lane):
    ahead = [[pltpu.roll(piece, 1, axis=1) for piece in pair] for pair in vector]
    behind = [[pltpu.roll(piece, LANES - 1, axis=1) for piece in pair] for pair in vector]
    own = (1.0 - 2.0 * coupling - opposite) / coupling
    other = opposite / coupling
    blended = []
    for i in range(CDOF):
        pair = []
        for h in range(2):
            still = own * vector[i][h] + other * vector[i][1 - h]
            beside = jnp.where(first_lane, ahead[i][1 - h], ahead[i][h]) + jnp.where(
                last_lane, behind[i][1 - h], behind[i][h]
            )
            pair.append(still + beside)
        blended.append(pair)
    return [
        [
            (blocks[i][0][h] * blended[0][h] + blocks[i][1][h] * blended[1][h])
            + (blocks[i][2][h] * blended[2][h] + blocks[i][3][h] * blended[3][h])
            for h in range(2)
        ]
        for i in range(CDOF)
    ]


def chain_kernel(
    where_ref, gathered, inverse_ref, fine_ref, index_ref, matrix_ref, out, ends, jumps, blocks_ref
):
    slice_here = where_ref[0]
    part_here = where_ref[1]
    lane = lax.broadcasted_iota(jnp.int32, (8, LANES), 1)
    first_lane = lane == 0
    last_lane = lane == LANES - 1
    quarter = lax.broadcasted_iota(jnp.int32, (SLICES, LANES), 1) // COARSE_DEV

    def regrouped(kind):
        held = [[jnp.zeros((SLICES, LANES), f32) for _ in range(2)] for _ in range(CDOF)]
        for p in range(PARTS):
            rows = gathered[pl.ds(2 * p + kind, SLICES, stride=2 * PARTS), :]
            for i in range(CDOF):
                by = (p % 4 - i) * COARSE_DEV % LANES
                moved = rows if by == 0 else pltpu.roll(rows, by, axis=1)
                held[i][p // 4] = jnp.where(quarter == p % 4, moved, held[i][p // 4])
        return held

    finish = regrouped(0)
    start = regrouped(1)
    for i in range(CDOF):
        for h in range(2):
            ends[2 * i + h] = finish[i][h]
            jumps[2 * i + h] = start[i][h]
            for j in range(CDOF):
                blocks_ref[i, j, h] = coupling * jnp.broadcast_to(
                    inverse_ref[i, j : j + 1, lanes_of(h)], (8, LANES)
                )
    blocks = [
        [[blocks_ref[i, j, h] for h in range(2)] for j in range(CDOF)] for i in range(CDOF)
    ]
    row = lax.broadcasted_iota(jnp.int32, (8, LANES), 0)

    def jump_group(group, carry):
        rows = pl.ds(pl.multiple_of(group * 8, 8), 8)
        vector = [[jumps[2 * i + h, rows, :] for h in range(2)] for i in range(CDOF)]
        for repeat in range(COARSE_STEPS):
            vector = coarse_step(vector, blocks, first_lane, last_lane)
        kept = (group > 0) | (row > 0)
        for i in range(CDOF):
            for h in range(2):
                jumps[2 * i + h, rows, :] = ends[2 * i + h, rows, :] - jnp.where(
                    kept, vector[i][h], 0.0
                )
        return carry

    lax.fori_loop(0, SLICES // 8, jump_group, 0)

    def row_of(ref, n, i, h):
        return jnp.broadcast_to(ref[2 * i + h, pl.ds(n, 1), :], (8, LANES))

    def link(n, flat):
        vector = [[flat[2 * i + h] for h in range(2)] for i in range(CDOF)]
        for repeat in range(COARSE_STEPS):
            vector = coarse_step(vector, blocks, first_lane, last_lane)
        return tuple(
            vector[i][h] + row_of(jumps, n, i, h) for i in range(CDOF) for h in range(2)
        )

    chain = lax.fori_loop(
        1,
        slice_here + 1,
        link,
        tuple(row_of(jumps, 0, i, h) for i in range(CDOF) for h in range(2)),
    )
    upper = part_here >= PARTS // 2
    spread = jnp.zeros((ROWS, LANES), f32)
    for i in range(CDOF):
        change = [chain[2 * i + h] - row_of(ends, slice_here, i, h) for h in range(2)]
        chosen = jnp.where(upper, change[1], change[0])
        spread = spread + matrix_ref[:, i : i + 1] * jnp.concatenate([chosen] * 3, axis=0)
    members = (
        lax.broadcasted_iota(jnp.int32, (LANES, CELLS_DEV), 0)
        == index_ref[...] + COARSE_DEV * (part_here % 4)
    ).astype(f32).astype(bf16)
    total = fine_ref[...]
    first, rest = two_terms(spread)
    second, third = two_terms(spread - first.astype(f32))
    for term in (third, second, first):
        total = total + jnp.dot(term, members, preferred_element_type=f32)
    out[0] = total[0:DOF]


def march_scratch():
    width = (WINDOW + 2) * LANES
    return [
        pltpu.VMEM((ROWS, width), f32),
        pltpu.VMEM((ROWS, width), f32),
        pltpu.VMEM((3, 8, width), jnp.int32),
        pltpu.VMEM((10, 8, width), f32),
    ]


params = pltpu.CompilerParams(vmem_limit_bytes=32 * 1024 * 1024)


def both_sides(values):
    ring = [(i, (i + 1) % PARTS) for i in range(PARTS)]
    back = [((i + 1) % PARTS, i) for i in range(PARTS)]
    return lax.ppermute(values, "space", ring), lax.ppermute(values, "space", back)


def local(
    states,
    neighbour,
    edge_x,
    edge_y,
    edge_damp,
    coriolis,
    flux_x,
    flux_y,
    rotation,
    restrict_matrix,
    prolong_matrix,
    restrict_index,
    coarse_inverse,
):
    pack = jnp.concatenate(
        [states[0], neighbour.astype(f32), edge_x, edge_y, edge_damp, coriolis[None, :]], axis=0
    )
    left, right = both_sides(pack)
    wide = [jnp.pad(m, ((0, ROWS - DOF), (0, ROWS - DOF))) for m in (flux_x, flux_y, rotation)]
    stencil = jnp.concatenate(wide + [jnp.zeros((ROWS, 8), f32)], axis=1)
    high = stencil.astype(bf16)
    low = (stencil - lax.reduce_precision(stencil, 8, 7)).astype(bf16)
    stencil_terms = jnp.concatenate([high, high, low], axis=1)
    index_row = restrict_index[None, :]

    half = pl.pallas_call(
        first_phase_kernel,
        out_shape=jax.ShapeDtypeStruct((ROWS, CELLS_DEV), f32),
        in_specs=[vmem] * 4,
        out_specs=vmem,
        scratch_shapes=march_scratch(),
        compiler_params=params,
    )(left, pack, right, stencil_terms)
    half_left, half_right = both_sides(half)
    fine, message = pl.pallas_call(
        second_phase_kernel,
        out_shape=(
            jax.ShapeDtypeStruct((ROWS, CELLS_DEV), f32),
            jax.ShapeDtypeStruct((2, LANES), f32),
        ),
        in_specs=[vmem] * 9,
        out_specs=(vmem, vmem),
        scratch_shapes=march_scratch(),
        compiler_params=params,
    )(half_left, half, half_right, left, pack, right, stencil_terms, index_row, restrict_matrix)

    copies = jnp.broadcast_to(message, (SLICES * PARTS, 2, LANES))
    gathered = lax.all_to_all(copies, ("tm", "space"), 0, 0, tiled=True)
    gathered = gathered.reshape(SLICES * PARTS * 2, LANES)
    where = jnp.stack([lax.axis_index("tm"), lax.axis_index("space")]).astype(jnp.int32)
    spread_matrix = jnp.pad(prolong_matrix, ((0, ROWS - DOF), (0, 0)))
    return pl.pallas_call(
        chain_kernel,
        out_shape=jax.ShapeDtypeStruct((1, DOF, CELLS_DEV), f32),
        in_specs=[pl.BlockSpec(memory_space=pltpu.SMEM)] + [vmem] * 5,
        out_specs=vmem,
        scratch_shapes=[
            pltpu.VMEM((2 * CDOF, SLICES, LANES), f32),
            pltpu.VMEM((2 * CDOF, SLICES, LANES), f32),
            pltpu.VMEM((CDOF, CDOF, 2, 8, LANES), f32),
        ],
        compiler_params=params,
    )(where, gathered, coarse_inverse, fine, index_row, spread_matrix)


def solution(mesh):
    in_specs = (
        P("tm", None, "space"),
        P(None, "space"),
        P(None, "space"),
        P(None, "space"),
        P(None, "space"),
        P("space"),
        P(),
        P(),
        P(),
        P(),
        P(),
        P("space"),
        P(),
    )
    out_specs = P("tm", None, "space")
    return jax.shard_map(local, mesh=mesh, in_specs=in_specs, out_specs=out_specs, check_vma=False)
```

```python
import functools

import jax
import jax.numpy as jnp
from jax import lax
from jax.experimental import pallas as pl
from jax.experimental.pallas import tpu as pltpu
from jax.sharding import PartitionSpec as P

DOF = 21
CDOF = 4
ROWS = 24
LANES = 128
HALF = 64
CELLS_DEV = 1024
COARSE_DEV = 32
COARSE_STEPS = 4
PARTS = 8
SLICES = 64
GROUP = 8
GROUPS = SLICES // GROUP
BLOCKS = CELLS_DEV // LANES
PHASE_STEPS = 8
SEGMENT = 2
WINDOW = 3 * BLOCKS

coupling = 0.1
opposite = 0.25
highest = lax.Precision.HIGHEST
f32 = jnp.float32
bf16 = jnp.bfloat16
vmem = pl.BlockSpec(memory_space=pltpu.VMEM)


def lane_gather(values, index):
    numbers = lax.GatherDimensionNumbers(
        offset_dims=(),
        collapsed_slice_dims=(1,),
        start_index_map=(1,),
        operand_batching_dims=(0,),
        start_indices_batching_dims=(0,),
    )
    return lax.gather(
        values, index[..., None], numbers, (1, 1), mode=lax.GatherScatterMode.PROMISE_IN_BOUNDS
    )


def two_terms(values):
    high = values.astype(bf16)
    return high, (values - high.astype(f32)).astype(bf16)


def lanes_of(block, count=1):
    return slice(block * LANES, (block + count) * LANES)


def fill_window(state_refs, mesh_refs, field, places, coefs):
    inside = lax.broadcasted_iota(jnp.int32, (ROWS, CELLS_DEV), 0) < DOF
    lane = lax.broadcasted_iota(jnp.int32, (8, CELLS_DEV), 1) % LANES
    edge = jnp.zeros((ROWS, LANES), f32)
    field[:, lanes_of(0)] = edge
    field[:, lanes_of(WINDOW + 1)] = edge
    for part, (state_ref, mesh_ref) in enumerate(zip(state_refs, mesh_refs)):
        cells = lanes_of(1 + part * BLOCKS, BLOCKS)
        field[:, cells] = jnp.where(inside, state_ref[0:ROWS, :], 0.0)
        for e in range(3):
            offset = mesh_ref[DOF + e : DOF + e + 1, :].astype(jnp.int32)
            target = jnp.broadcast_to(offset, (8, CELLS_DEV)) + lane
            within = (target >= 0) & (target < LANES)
            places[e, :, cells] = (target & (LANES - 1)) + jnp.where(within, 0, LANES)
        for row in range(10):
            coefs[row, :, cells] = jnp.broadcast_to(
                mesh_ref[DOF + 3 + row : DOF + 4 + row, :], (8, CELLS_DEV)
            )


def block_rate(source, block, places, coefs, stencil, low_half):
    here = lanes_of(block)
    centre = []
    around = []
    for r in range(3):
        rows = slice(8 * r, 8 * r + 8)
        centre.append(source[rows, here])
        around.append(
            jnp.where(low_half, source[rows, lanes_of(block + 1)], source[rows, lanes_of(block - 1)])
        )
    sums = [[None] * 3 for _ in range(3)]
    for e in range(3):
        place = places[e, :, here]
        index = place & (LANES - 1)
        within = place < LANES
        found = [lane_gather(piece, index) for piece in centre + around]
        for r in range(3):
            difference = jnp.where(within, found[r], found[3 + r]) - centre[r]
            for a in range(3):
                term = coefs[3 * a + e, :, here] * difference
                sums[a][r] = term if e == 0 else sums[a][r] + term
    turned = [coefs[9, :, here] * piece for piece in centre]
    stacked = jnp.concatenate(sums[0] + sums[1] + turned + [jnp.zeros((8, LANES), f32)], axis=0)
    high, low = two_terms(stacked)
    mixed = jnp.dot(
        stencil, jnp.concatenate([high, low, high], axis=0), preferred_element_type=f32
    )
    return mixed + jnp.concatenate(sums[2], axis=0)


def march(field, middle, places, coefs, stencil_ref):
    low_half = lax.broadcasted_iota(jnp.int32, (8, LANES), 1) < HALF
    edge = jnp.zeros((ROWS, LANES), f32)
    middle[:, lanes_of(0)] = edge
    middle[:, lanes_of(WINDOW + 1)] = edge

    for first in range(0, PHASE_STEPS, SEGMENT):
        blocks = range(1 + first, 1 + WINDOW - first)

        def step(index, carry):
            stencil = stencil_ref[...]
            for b in blocks:
                rate = block_rate(field, b, places, coefs, stencil, low_half)
                middle[:, lanes_of(b)] = field[:, lanes_of(b)] + rate
            for b in blocks:
                rate = block_rate(middle, b, places, coefs, stencil, low_half)
                here = lanes_of(b)
                field[:, here] = 0.5 * (field[:, here] + middle[:, here] + rate)
            return carry

        lax.fori_loop(0, SEGMENT, step, 0)


def first_phase_kernel(left, centre, right, stencil_ref, out, field, middle, places, coefs):
    packs = (left, centre, right)
    fill_window(packs, packs, field, places, coefs)
    march(field, middle, places, coefs, stencil_ref)
    out[...] = field[:, lanes_of(1 + BLOCKS, BLOCKS)]


def restricted(values, members, restrict_matrix):
    contract = (((1,), (1,)), ((), ()))
    first, rest = two_terms(values)
    second, third = two_terms(values - first.astype(f32))
    totals = jnp.zeros((ROWS, COARSE_DEV), f32)
    for term in (third, second, first):
        totals = totals + lax.dot_general(term, members, contract, preferred_element_type=f32)
    counts = lax.dot_general(
        jnp.ones((16, CELLS_DEV), bf16), members, contract, preferred_element_type=f32
    )[0:1]
    result = jnp.zeros((CDOF, COARSE_DEV), f32)
    for d in range(DOF):
        result = result + restrict_matrix[:, d : d + 1] * totals[d : d + 1, :]
    return result / counts


def in_one_row(coarse):
    return jnp.concatenate([coarse[i : i + 1, :] for i in range(CDOF)], axis=1)


def second_phase_kernel(
    left, centre, right, left_mesh, centre_mesh, right_mesh, stencil_ref, index_ref, matrix_ref,
    out, message, field, middle, places, coefs,
):
    fill_window(
        (left, centre, right), (left_mesh, centre_mesh, right_mesh), field, places, coefs
    )
    march(field, middle, places, coefs, stencil_ref)
    fine = field[:, lanes_of(1 + BLOCKS, BLOCKS)]
    out[...] = fine
    members = (
        lax.broadcasted_iota(jnp.int32, (COARSE_DEV, CELLS_DEV), 0) == index_ref[...]
    ).astype(f32).astype(bf16)
    matrix = matrix_ref[...]
    inside = lax.broadcasted_iota(jnp.int32, (ROWS, CELLS_DEV), 0) < DOF
    start = jnp.where(inside, centre_mesh[0:ROWS, :], 0.0)
    rows = jnp.concatenate(
        [in_one_row(restricted(fine, members, matrix)), in_one_row(restricted(start, members, matrix))],
        axis=0,
    )
    for copy in range(GROUP * PARTS):
        message[copy] = rows


def flipped(tiles, even_row):
    up = pltpu.roll(jnp.concatenate([tiles[1:], tiles[:1]], axis=0), 7, axis=1)
    down = pltpu.roll(jnp.concatenate([tiles[7:], tiles[:7]], axis=0), 1, axis=1)
    return jnp.where(even_row, up, down)


def compose_kernel(inverse_ref, out):
    shape = (8, 8, LANES)
    row = lax.broadcasted_iota(jnp.int32, shape, 1)
    lane = lax.broadcasted_iota(jnp.int32, shape, 2)
    turn = lax.broadcasted_iota(jnp.int32, shape, 0)
    even_row = row % 2 == 0
    first_lane = lane == 0
    last_lane = lane == LANES - 1
    own = 1.0 - 2.0 * coupling - opposite
    blocks = []
    for by in range(CDOF):
        pieces = []
        for i in range(CDOF):
            j = (i - by) % CDOF
            for h in range(2):
                pieces.append(inverse_ref[i, j : j + 1, lanes_of(h)])
        blocks.append(jnp.concatenate(pieces, axis=0)[None])
    reach = {0: jnp.where(turn == 0, 1.0, 0.0)}
    for repeat in range(COARSE_STEPS):
        swapped = {o: flipped(tiles, even_row) for o, tiles in reach.items()}
        blended = {}
        for o in range(-repeat - 1, repeat + 2):
            total = jnp.zeros(shape, f32)
            if o in reach:
                total = own * reach[o] + opposite * swapped[o]
            if o - 1 in reach:
                edge = jnp.where(last_lane, swapped[o - 1], reach[o - 1])
                total = total + coupling * pltpu.roll(edge, 1, axis=2)
            if o + 1 in reach:
                edge = jnp.where(first_lane, swapped[o + 1], reach[o + 1])
                total = total + coupling * pltpu.roll(edge, LANES - 1, axis=2)
            blended[o] = total
        reach = {}
        for o, tiles in blended.items():
            total = blocks[0] * tiles
            for by in range(1, CDOF):
                turned = jnp.concatenate([tiles[8 - 2 * by :], tiles[: 8 - 2 * by]], axis=0)
                total = total + blocks[by] * pltpu.roll(turned, 2 * by, axis=1)
            reach[o] = total
    for o, tiles in reach.items():
        out[o + COARSE_STEPS] = tiles if o == 0 else pltpu.roll(tiles, -o % LANES, axis=2)


def added(terms):
    while len(terms) > 1:
        terms = [sum(terms[i : i + 2][1:], terms[i]) for i in range(0, len(terms), 2)]
    return terms[0]


def coarse_slice(vector, operator_ref):
    turns = [vector] + [pltpu.roll(vector, d, axis=0) for d in range(1, 8)]
    shares = []
    for o in range(-COARSE_STEPS, COARSE_STEPS + 1):
        share = added([operator_ref[o + COARSE_STEPS, d] * turns[d] for d in range(8)])
        shares.append(share if o == 0 else pltpu.roll(share, o % LANES, axis=1))
    return added(shares)


def group_kernel(where_ref, gathered, operator_ref, ends_out, own_out, finish, start):
    group = where_ref[0]
    place = where_ref[1]
    quarter = lax.broadcasted_iota(jnp.int32, (GROUP, LANES), 1) // COARSE_DEV
    for kind, ref in enumerate((finish, start)):
        for i in range(CDOF):
            for h in range(2):
                held = jnp.zeros((GROUP, LANES), f32)
                for q in range(4):
                    p = 4 * h + q
                    rows = gathered[pl.ds(2 * p + kind, GROUP, stride=2 * PARTS), :]
                    by = (q - i) * COARSE_DEV % LANES
                    moved = rows if by == 0 else pltpu.roll(rows, by, axis=1)
                    held = jnp.where(quarter == q, moved, held)
                ref[pl.ds((2 * i + h) * GROUP, GROUP), :] = held

    def of_slice(ref, n):
        return ref[pl.ds(n, 8, stride=GROUP), :]

    chain = None
    own = jnp.zeros((8, LANES), f32)
    for n in range(GROUP):
        coarse = coarse_slice(of_slice(start, n), operator_ref)
        if n == 0:
            coarse = jnp.where(group > 0, coarse, 0.0)
        jump = of_slice(finish, n) - coarse
        chain = jump if n == 0 else coarse_slice(chain, operator_ref) + jump
        own = jnp.where(place == n, chain, own)
    for copy in range(GROUPS):
        ends_out[copy] = chain
    own_out[0] = own
    own_out[1] = finish[pl.ds(place, 8, stride=GROUP), :]


def correct_kernel(
    where_ref, ends, own_ref, operator_ref, fine_ref, index_ref, matrix_ref, out
):
    group = where_ref[0]
    place = where_ref[1]
    part = where_ref[2]

    def advance(count, vector):
        return lax.fori_loop(0, count, lambda n, now: coarse_slice(now, operator_ref), vector)

    def link(k, vector):
        return advance(GROUP, vector) + ends[k]

    before = lax.fori_loop(1, group, link, ends[0])
    before = advance(jnp.where(group > 0, place + 1, 0), before)
    chain = own_ref[0] + jnp.where(group > 0, before, 0.0)
    change = chain - own_ref[1]
    upper = part >= PARTS // 2
    spread = jnp.zeros((ROWS, LANES), f32)
    for i in range(CDOF):
        chosen = jnp.where(upper, change[2 * i + 1 : 2 * i + 2], change[2 * i : 2 * i + 1])
        spread = spread + matrix_ref[:, i : i + 1] * jnp.broadcast_to(chosen, (ROWS, LANES))
    members = (
        lax.broadcasted_iota(jnp.int32, (LANES, CELLS_DEV), 0)
        == index_ref[...] + COARSE_DEV * (part % 4)
    ).astype(f32).astype(bf16)
    total = fine_ref[...]
    first, rest = two_terms(spread)
    second, third = two_terms(spread - first.astype(f32))
    for term in (third, second, first):
        total = total + jnp.dot(term, members, preferred_element_type=f32)
    for d in range(DOF):
        out[d] = total[d : d + 1, :]


def march_scratch():
    width = (WINDOW + 2) * LANES
    return [
        pltpu.VMEM((ROWS, width), f32),
        pltpu.VMEM((ROWS, width), f32),
        pltpu.VMEM((3, 8, width), jnp.int32),
        pltpu.VMEM((10, 8, width), f32),
    ]


params = pltpu.CompilerParams(vmem_limit_bytes=32 * 1024 * 1024)


def both_sides(values):
    ring = [(i, (i + 1) % PARTS) for i in range(PARTS)]
    back = [((i + 1) % PARTS, i) for i in range(PARTS)]
    return lax.ppermute(values, "space", ring), lax.ppermute(values, "space", back)


def local(
    states,
    neighbour,
    edge_x,
    edge_y,
    edge_damp,
    coriolis,
    flux_x,
    flux_y,
    rotation,
    restrict_matrix,
    prolong_matrix,
    restrict_index,
    coarse_inverse,
):
    pack = jnp.concatenate(
        [states[0], neighbour.astype(f32), edge_x, edge_y, edge_damp, coriolis[None, :]], axis=0
    )
    left, right = both_sides(pack)
    wide = [jnp.pad(m, ((0, ROWS - DOF), (0, ROWS - DOF))) for m in (flux_x, flux_y, rotation)]
    stencil = jnp.concatenate(wide + [jnp.zeros((ROWS, 8), f32)], axis=1)
    high = stencil.astype(bf16)
    low = (stencil - lax.reduce_precision(stencil, 8, 7)).astype(bf16)
    stencil_terms = jnp.concatenate([high, high, low], axis=1)
    index_row = restrict_index[None, :]
    operator = pl.pallas_call(
        compose_kernel,
        out_shape=jax.ShapeDtypeStruct((2 * COARSE_STEPS + 1, 8, 8, LANES), f32),
        in_specs=[vmem],
        out_specs=vmem,
        compiler_params=params,
        cost_estimate=pl.CostEstimate(flops=4000000, bytes_accessed=300000, transcendentals=0),
    )(coarse_inverse)

    half = pl.pallas_call(
        first_phase_kernel,
        out_shape=jax.ShapeDtypeStruct((ROWS, CELLS_DEV), f32),
        in_specs=[vmem] * 4,
        out_specs=vmem,
        scratch_shapes=march_scratch(),
        compiler_params=params,
    )(left, pack, right, stencil_terms)
    half_left, half_right = both_sides(half)
    fine, message = pl.pallas_call(
        second_phase_kernel,
        out_shape=(
            jax.ShapeDtypeStruct((ROWS, CELLS_DEV), f32),
            jax.ShapeDtypeStruct((GROUP * PARTS, 2, LANES), f32),
        ),
        in_specs=[vmem] * 9,
        out_specs=(vmem, vmem),
        scratch_shapes=march_scratch(),
        compiler_params=params,
    )(half_left, half, half_right, left, pack, right, stencil_terms, index_row, restrict_matrix)

    axes = ("tm", "space")
    members = GROUP * PARTS
    inside = [[g * members + m for m in range(members)] for g in range(GROUPS)]
    across = [[g * members + m for g in range(GROUPS)] for m in range(members)]
    gathered = lax.all_to_all(message, axes, 0, 0, tiled=True, axis_index_groups=inside)
    slice_here = lax.axis_index("tm")
    where = jnp.stack([slice_here // GROUP, slice_here % GROUP, lax.axis_index("space")])
    where = where.astype(jnp.int32)
    smem = pl.BlockSpec(memory_space=pltpu.SMEM)
    ends, own = pl.pallas_call(
        group_kernel,
        out_shape=(
            jax.ShapeDtypeStruct((GROUPS, 8, LANES), f32),
            jax.ShapeDtypeStruct((2, 8, LANES), f32),
        ),
        in_specs=[smem, vmem, vmem],
        out_specs=(vmem, vmem),
        scratch_shapes=[pltpu.VMEM((8 * GROUP, LANES), f32)] * 2,
        compiler_params=params,
    )(where, gathered.reshape(GROUP * PARTS * 2, LANES), operator)
    ends = lax.all_to_all(ends, axes, 0, 0, tiled=True, axis_index_groups=across)
    spread_matrix = jnp.pad(prolong_matrix, ((0, ROWS - DOF), (0, 0)))
    updated = pl.pallas_call(
        correct_kernel,
        out_shape=jax.ShapeDtypeStruct((DOF, 1, CELLS_DEV), f32),
        in_specs=[smem] + [vmem] * 6,
        out_specs=vmem,
        compiler_params=params,
    )(where, ends, own, operator, fine, index_row, spread_matrix)
    return updated.transpose(1, 0, 2)


def solution(mesh):
    in_specs = (
        P("tm", None, "space"),
        P(None, "space"),
        P(None, "space"),
        P(None, "space"),
        P(None, "space"),
        P("space"),
        P(),
        P(),
        P(),
        P(),
        P(),
        P("space"),
        P(),
    )
    out_specs = P("tm", None, "space")
    return jax.shard_map(local, mesh=mesh, in_specs=in_specs, out_specs=out_specs, check_vma=False)
```

```python
import functools

import jax
import jax.numpy as jnp
from jax import lax
from jax.experimental import pallas as pl
from jax.experimental.pallas import tpu as pltpu
from jax.sharding import PartitionSpec as P

DOF = 21
CDOF = 4
ROWS = 24
LANES = 128
HALF = 64
CELLS_DEV = 1024
COARSE_DEV = 32
COARSE_STEPS = 4
PARTS = 8
SLICES = 64
GROUP = 8
GROUPS = SLICES // GROUP
BLOCKS = CELLS_DEV // LANES
PHASE_STEPS = 8
WINDOW = 3 * BLOCKS

coupling = 0.1
opposite = 0.25
highest = lax.Precision.HIGHEST
f32 = jnp.float32
bf16 = jnp.bfloat16
vmem = pl.BlockSpec(memory_space=pltpu.VMEM)


def lane_gather(values, index):
    numbers = lax.GatherDimensionNumbers(
        offset_dims=(),
        collapsed_slice_dims=(1,),
        start_index_map=(1,),
        operand_batching_dims=(0,),
        start_indices_batching_dims=(0,),
    )
    return lax.gather(
        values, index[..., None], numbers, (1, 1), mode=lax.GatherScatterMode.PROMISE_IN_BOUNDS
    )


def two_terms(values):
    high = values.astype(bf16)
    return high, (values - high.astype(f32)).astype(bf16)


def lanes_of(block, count=1):
    return slice(block * LANES, (block + count) * LANES)


def sides(odd, first, second, rows):
    one, two = first[rows, :], second[rows, :]
    return jnp.where(odd, one, two), jnp.where(odd, two, one)


def fill_window(odd, state_refs, mesh_refs, field, places, coefs):
    inside = lax.broadcasted_iota(jnp.int32, (ROWS, CELLS_DEV), 0) < DOF
    lane = lax.broadcasted_iota(jnp.int32, (8, CELLS_DEV), 1) % LANES
    edge = jnp.zeros((ROWS, LANES), f32)
    field[:, lanes_of(0)] = edge
    field[:, lanes_of(WINDOW + 1)] = edge

    def in_order(refs, rows):
        left, right = sides(odd, refs[0], refs[2], rows)
        return left, refs[1][rows, :], right

    for part, state in enumerate(in_order(state_refs, slice(0, ROWS))):
        field[:, lanes_of(1 + part * BLOCKS, BLOCKS)] = jnp.where(inside, state, 0.0)
    for part, mesh in enumerate(in_order(mesh_refs, slice(DOF, DOF + 13))):
        cells = lanes_of(1 + part * BLOCKS, BLOCKS)
        for e in range(3):
            offset = mesh[e : e + 1, :].astype(jnp.int32)
            target = jnp.broadcast_to(offset, (8, CELLS_DEV)) + lane
            within = (target >= 0) & (target < LANES)
            places[e, :, cells] = (target & (LANES - 1)) + jnp.where(within, 0, LANES)
        for row in range(10):
            coefs[row, :, cells] = jnp.broadcast_to(mesh[3 + row : 4 + row, :], (8, CELLS_DEV))


def block_rate(source, block, places, coefs, stencil, low_half):
    here = lanes_of(block)
    centre = []
    around = []
    for r in range(3):
        rows = slice(8 * r, 8 * r + 8)
        centre.append(source[rows, here])
        around.append(
            jnp.where(low_half, source[rows, lanes_of(block + 1)], source[rows, lanes_of(block - 1)])
        )
    sums = [[None] * 3 for _ in range(3)]
    for e in range(3):
        place = places[e, :, here]
        index = place & (LANES - 1)
        within = place < LANES
        found = [lane_gather(piece, index) for piece in centre + around]
        for r in range(3):
            difference = jnp.where(within, found[r], found[3 + r]) - centre[r]
            for a in range(3):
                term = coefs[3 * a + e, :, here] * difference
                sums[a][r] = term if e == 0 else sums[a][r] + term
    turned = [coefs[9, :, here] * piece for piece in centre]
    stacked = jnp.concatenate(sums[0] + sums[1] + turned + [jnp.zeros((8, LANES), f32)], axis=0)
    high, low = two_terms(stacked)
    mixed = jnp.dot(
        stencil, jnp.concatenate([high, low, high], axis=0), preferred_element_type=f32
    )
    return mixed + jnp.concatenate(sums[2], axis=0)


def march(field, middle, places, coefs, stencil_ref):
    low_half = lax.broadcasted_iota(jnp.int32, (8, LANES), 1) < HALF
    edge = jnp.zeros((ROWS, LANES), f32)
    middle[:, lanes_of(0)] = edge
    middle[:, lanes_of(WINDOW + 1)] = edge

    stencil = stencil_ref[...]
    for index in range(PHASE_STEPS):
        for b in range(1 + index, 1 + WINDOW - index):
            rate = block_rate(field, b, places, coefs, stencil, low_half)
            middle[:, lanes_of(b)] = field[:, lanes_of(b)] + rate
        for b in range(2 + index, WINDOW - index):
            rate = block_rate(middle, b, places, coefs, stencil, low_half)
            here = lanes_of(b)
            field[:, here] = 0.5 * (field[:, here] + middle[:, here] + rate)


def first_phase_kernel(
    where_ref, first, centre, second, stencil_ref, out, field, middle, places, coefs
):
    packs = (first, centre, second)
    fill_window(where_ref[2] % 2 == 1, packs, packs, field, places, coefs)
    march(field, middle, places, coefs, stencil_ref)
    out[...] = field[:, lanes_of(1 + BLOCKS, BLOCKS)]


def restricted(values, index_row, restrict_matrix):
    members = (
        lax.broadcasted_iota(jnp.int32, (COARSE_DEV, CELLS_DEV), 0) == index_row
    ).astype(f32).astype(bf16)
    contract = (((1,), (1,)), ((), ()))
    totals = jnp.zeros((ROWS, COARSE_DEV), f32)
    for term in two_terms(values):
        totals = totals + lax.dot_general(term, members, contract, preferred_element_type=f32)
    counts = lax.dot_general(
        jnp.ones((16, CELLS_DEV), bf16), members, contract, preferred_element_type=f32
    )[0:1]
    result = jnp.zeros((CDOF, COARSE_DEV), f32)
    for d in range(DOF):
        result = result + restrict_matrix[:, d : d + 1] * totals[d : d + 1, :]
    result = result / counts
    return jnp.concatenate([result[i : i + 1, :] for i in range(CDOF)], axis=1)


def start_kernel(pack_ref, index_ref, matrix_ref, out):
    inside = lax.broadcasted_iota(jnp.int32, (ROWS, CELLS_DEV), 0) < DOF
    start = jnp.where(inside, pack_ref[0:ROWS, :], 0.0)
    out[...] = restricted(start, index_ref[...], matrix_ref[...])


def second_phase_kernel(
    where_ref, first, centre, second, first_mesh, centre_mesh, second_mesh, stencil_ref, index_ref,
    matrix_ref, start_ref, out, message, field, middle, places, coefs,
):
    odd = where_ref[2] % 2 == 1
    mesh_refs = (first_mesh, centre_mesh, second_mesh)
    fill_window(odd, (first, centre, second), mesh_refs, field, places, coefs)
    march(field, middle, places, coefs, stencil_ref)
    fine = field[:, lanes_of(1 + BLOCKS, BLOCKS)]
    out[...] = fine
    rows = jnp.concatenate(
        [restricted(fine, index_ref[...], matrix_ref[...]), start_ref[...]], axis=0
    )
    for copy in range(GROUP * PARTS):
        message[copy] = rows


def flipped(tiles, even_row):
    up = pltpu.roll(jnp.concatenate([tiles[1:], tiles[:1]], axis=0), 7, axis=1)
    down = pltpu.roll(jnp.concatenate([tiles[7:], tiles[:7]], axis=0), 1, axis=1)
    return jnp.where(even_row, up, down)


def compose_kernel(inverse_ref, out, out_twice):
    shape = (8, 8, LANES)
    row = lax.broadcasted_iota(jnp.int32, shape, 1)
    lane = lax.broadcasted_iota(jnp.int32, shape, 2)
    turn = lax.broadcasted_iota(jnp.int32, shape, 0)
    even_row = row % 2 == 0
    first_lane = lane == 0
    last_lane = lane == LANES - 1
    own = 1.0 - 2.0 * coupling - opposite
    blocks = []
    for by in range(CDOF):
        pieces = []
        for i in range(CDOF):
            j = (i - by) % CDOF
            for h in range(2):
                pieces.append(inverse_ref[i, j : j + 1, lanes_of(h)])
        blocks.append(jnp.concatenate(pieces, axis=0)[None])
    reach = {0: jnp.where(turn == 0, 1.0, 0.0)}
    for repeat in range(2 * COARSE_STEPS):
        swapped = {o: flipped(tiles, even_row) for o, tiles in reach.items()}
        blended = {}
        for o in range(-repeat - 1, repeat + 2):
            total = jnp.zeros(shape, f32)
            if o in reach:
                total = own * reach[o] + opposite * swapped[o]
            if o - 1 in reach:
                edge = jnp.where(last_lane, swapped[o - 1], reach[o - 1])
                total = total + coupling * pltpu.roll(edge, 1, axis=2)
            if o + 1 in reach:
                edge = jnp.where(first_lane, swapped[o + 1], reach[o + 1])
                total = total + coupling * pltpu.roll(edge, LANES - 1, axis=2)
            blended[o] = total
        reach = {}
        for o, tiles in blended.items():
            total = blocks[0] * tiles
            for by in range(1, CDOF):
                turned = jnp.concatenate([tiles[8 - 2 * by :], tiles[: 8 - 2 * by]], axis=0)
                total = total + blocks[by] * pltpu.roll(turned, 2 * by, axis=1)
            reach[o] = total
        if (repeat + 1) % COARSE_STEPS == 0:
            held = out if repeat < COARSE_STEPS else out_twice
            for o, tiles in reach.items():
                held[o + repeat + 1] = tiles if o == 0 else pltpu.roll(tiles, -o % LANES, axis=2)


def added(terms):
    while len(terms) > 1:
        terms = [sum(terms[i : i + 2][1:], terms[i]) for i in range(0, len(terms), 2)]
    return terms[0]


def coarse_slice(vector, operator_ref):
    turns = [vector] + [pltpu.roll(vector, d, axis=0) for d in range(1, 8)]
    reach = operator_ref.shape[0] // 2
    shares = []
    for o in range(-reach, reach + 1):
        share = added([operator_ref[o + reach, d] * turns[d] for d in range(8)])
        shares.append(share if o == 0 else pltpu.roll(share, o % LANES, axis=1))
    return added(shares)


def group_kernel(where_ref, gathered, operator_ref, ends_out, own_out, finish, start):
    group = where_ref[0]
    place = where_ref[1]
    quarter = lax.broadcasted_iota(jnp.int32, (GROUP, LANES), 1) // COARSE_DEV
    for kind, ref in enumerate((finish, start)):
        for i in range(CDOF):
            for h in range(2):
                held = jnp.zeros((GROUP, LANES), f32)
                for q in range(4):
                    p = 4 * h + q
                    rows = gathered[pl.ds(2 * p + kind, GROUP, stride=2 * PARTS), :]
                    by = (q - i) * COARSE_DEV % LANES
                    moved = rows if by == 0 else pltpu.roll(rows, by, axis=1)
                    held = jnp.where(quarter == q, moved, held)
                ref[pl.ds((2 * i + h) * GROUP, GROUP), :] = held

    def of_slice(ref, n):
        return ref[pl.ds(n, 8, stride=GROUP), :]

    chain = None
    own = jnp.zeros((8, LANES), f32)
    for n in range(GROUP):
        coarse = coarse_slice(of_slice(start, n), operator_ref)
        if n == 0:
            coarse = jnp.where(group > 0, coarse, 0.0)
        jump = of_slice(finish, n) - coarse
        chain = jump if n == 0 else coarse_slice(chain, operator_ref) + jump
        own = jnp.where(place == n, chain, own)
    for copy in range(GROUPS):
        ends_out[copy] = chain
    own_out[0] = own
    own_out[1] = finish[pl.ds(place, 8, stride=GROUP), :]


def correct_kernel(
    where_ref, ends, own_ref, operator_ref, twice_ref, fine_ref, index_ref, matrix_ref, out
):
    group = where_ref[0]
    place = where_ref[1]
    part = where_ref[2]

    def advance(count, vector, ref):
        return lax.fori_loop(0, count, lambda n, now: coarse_slice(now, ref), vector)

    def link(k, vector):
        return advance(GROUP // 2, vector, twice_ref) + ends[k]

    before = lax.fori_loop(1, group, link, ends[0])
    count = jnp.where(group > 0, place + 1, 0)
    before = advance(count % 2, advance(count // 2, before, twice_ref), operator_ref)
    chain = own_ref[0] + jnp.where(group > 0, before, 0.0)
    change = chain - own_ref[1]
    upper = part >= PARTS // 2
    spread = jnp.zeros((ROWS, LANES), f32)
    for i in range(CDOF):
        chosen = jnp.where(upper, change[2 * i + 1 : 2 * i + 2], change[2 * i : 2 * i + 1])
        spread = spread + matrix_ref[:, i : i + 1] * jnp.broadcast_to(chosen, (ROWS, LANES))
    members = (
        lax.broadcasted_iota(jnp.int32, (LANES, CELLS_DEV), 0)
        == index_ref[...] + COARSE_DEV * (part % 4)
    ).astype(f32).astype(bf16)
    total = fine_ref[...]
    for term in two_terms(spread):
        total = total + jnp.dot(term, members, preferred_element_type=f32)
    for d in range(DOF):
        out[d] = total[d : d + 1, :]


def march_scratch():
    width = (WINDOW + 2) * LANES
    return [
        pltpu.VMEM((ROWS, width), f32),
        pltpu.VMEM((ROWS, width), f32),
        pltpu.VMEM((3, 8, width), jnp.int32),
        pltpu.VMEM((10, 8, width), f32),
    ]


params = pltpu.CompilerParams(vmem_limit_bytes=32 * 1024 * 1024)


def both_sides(values):
    pairs = [(i, i ^ 1) for i in range(PARTS)]
    others = [(i, (((i + 1) ^ 1) - 1) % PARTS) for i in range(PARTS)]
    return lax.ppermute(values, "space", pairs), lax.ppermute(values, "space", others)


smem = pl.BlockSpec(memory_space=pltpu.SMEM)


def local(
    states,
    neighbour,
    edge_x,
    edge_y,
    edge_damp,
    coriolis,
    flux_x,
    flux_y,
    rotation,
    restrict_matrix,
    prolong_matrix,
    restrict_index,
    coarse_inverse,
):
    pack = jnp.concatenate(
        [states[0], neighbour.astype(f32), edge_x, edge_y, edge_damp, coriolis[None, :]], axis=0
    )
    first, second = both_sides(pack)
    slice_here = lax.axis_index("tm")
    where = jnp.stack([slice_here // GROUP, slice_here % GROUP, lax.axis_index("space")])
    where = where.astype(jnp.int32)
    wide = [jnp.pad(m, ((0, ROWS - DOF), (0, ROWS - DOF))) for m in (flux_x, flux_y, rotation)]
    stencil = jnp.concatenate(wide + [jnp.zeros((ROWS, 8), f32)], axis=1)
    high = stencil.astype(bf16)
    low = (stencil - lax.reduce_precision(stencil, 8, 7)).astype(bf16)
    stencil_terms = jnp.concatenate([high, high, low], axis=1)
    index_row = restrict_index[None, :]
    start = pl.pallas_call(
        start_kernel,
        out_shape=jax.ShapeDtypeStruct((1, LANES), f32),
        in_specs=[vmem] * 3,
        out_specs=vmem,
        compiler_params=params,
        cost_estimate=pl.CostEstimate(flops=4000000, bytes_accessed=200000, transcendentals=0),
    )(pack, index_row, restrict_matrix)

    half = pl.pallas_call(
        first_phase_kernel,
        out_shape=jax.ShapeDtypeStruct((ROWS, CELLS_DEV), f32),
        in_specs=[smem] + [vmem] * 4,
        out_specs=vmem,
        scratch_shapes=march_scratch(),
        compiler_params=params,
    )(where, first, pack, second, stencil_terms)
    half_first, half_second = both_sides(half)
    fine, message = pl.pallas_call(
        second_phase_kernel,
        out_shape=(
            jax.ShapeDtypeStruct((ROWS, CELLS_DEV), f32),
            jax.ShapeDtypeStruct((GROUP * PARTS, 2, LANES), f32),
        ),
        in_specs=[smem] + [vmem] * 10,
        out_specs=(vmem, vmem),
        scratch_shapes=march_scratch(),
        compiler_params=params,
    )(
        where, half_first, half, half_second, first, pack, second, stencil_terms, index_row,
        restrict_matrix, start,
    )

    late_inverse, message = lax.optimization_barrier((coarse_inverse, message))
    operator, operator_twice = pl.pallas_call(
        compose_kernel,
        out_shape=tuple(
            jax.ShapeDtypeStruct((2 * reach + 1, 8, 8, LANES), f32)
            for reach in (COARSE_STEPS, 2 * COARSE_STEPS)
        ),
        in_specs=[vmem],
        out_specs=(vmem, vmem),
        compiler_params=params,
        cost_estimate=pl.CostEstimate(flops=12000000, bytes_accessed=900000, transcendentals=0),
    )(late_inverse)
    axes = ("tm", "space")
    members = GROUP * PARTS
    inside = [[g * members + m for m in range(members)] for g in range(GROUPS)]
    across = [[g * members + m for g in range(GROUPS)] for m in range(members)]
    gathered = lax.all_to_all(message, axes, 0, 0, tiled=True, axis_index_groups=inside)
    ends, own = pl.pallas_call(
        group_kernel,
        out_shape=(
            jax.ShapeDtypeStruct((GROUPS, 8, LANES), f32),
            jax.ShapeDtypeStruct((2, 8, LANES), f32),
        ),
        in_specs=[smem, vmem, vmem],
        out_specs=(vmem, vmem),
        scratch_shapes=[pltpu.VMEM((8 * GROUP, LANES), f32)] * 2,
        compiler_params=params,
    )(where, gathered.reshape(GROUP * PARTS * 2, LANES), operator)
    ends = lax.all_to_all(ends, axes, 0, 0, tiled=True, axis_index_groups=across)
    spread_matrix = jnp.pad(prolong_matrix, ((0, ROWS - DOF), (0, 0)))
    updated = pl.pallas_call(
        correct_kernel,
        out_shape=jax.ShapeDtypeStruct((DOF, 1, CELLS_DEV), f32),
        in_specs=[smem] + [vmem] * 7,
        out_specs=vmem,
        compiler_params=params,
    )(where, ends, own, operator, operator_twice, fine, index_row, spread_matrix)
    return updated.transpose(1, 0, 2)


def solution(mesh):
    in_specs = (
        P("tm", None, "space"),
        P(None, "space"),
        P(None, "space"),
        P(None, "space"),
        P(None, "space"),
        P("space"),
        P(),
        P(),
        P(),
        P(),
        P(),
        P("space"),
        P(),
    )
    out_specs = P("tm", None, "space")
    return jax.shard_map(local, mesh=mesh, in_specs=in_specs, out_specs=out_specs, check_vma=False)
```

```python
import functools

import jax
import jax.numpy as jnp
from jax import lax
from jax.experimental import pallas as pl
from jax.experimental.pallas import tpu as pltpu
from jax.sharding import PartitionSpec as P

DOF = 21
CDOF = 4
ROWS = 24
LANES = 128
HALF = 64
CELLS_DEV = 1024
COARSE_DEV = 32
COARSE_STEPS = 4
PARTS = 8
SLICES = 64
GROUP = 8
GROUPS = SLICES // GROUP
BLOCKS = CELLS_DEV // LANES
PHASE_STEPS = 8
WINDOW = 3 * BLOCKS

coupling = 0.1
opposite = 0.25
highest = lax.Precision.HIGHEST
f32 = jnp.float32
bf16 = jnp.bfloat16
vmem = pl.BlockSpec(memory_space=pltpu.VMEM)


def lane_gather(values, index):
    numbers = lax.GatherDimensionNumbers(
        offset_dims=(),
        collapsed_slice_dims=(1,),
        start_index_map=(1,),
        operand_batching_dims=(0,),
        start_indices_batching_dims=(0,),
    )
    return lax.gather(
        values, index[..., None], numbers, (1, 1), mode=lax.GatherScatterMode.PROMISE_IN_BOUNDS
    )


def two_terms(values):
    high = values.astype(bf16)
    return high, (values - high.astype(f32)).astype(bf16)


def lanes_of(block, count=1):
    return slice(block * LANES, (block + count) * LANES)


def sides(odd, first, second, rows):
    one, two = first[rows, :], second[rows, :]
    return jnp.where(odd, one, two), jnp.where(odd, two, one)


def in_order(odd, refs, rows):
    left, right = sides(odd, refs[0], refs[2], rows)
    return left, refs[1][rows, :], right


def fill_field(odd, state_refs, field):
    inside = lax.broadcasted_iota(jnp.int32, (ROWS, CELLS_DEV), 0) < DOF
    edge = jnp.zeros((ROWS, LANES), f32)
    field[:, lanes_of(0)] = edge
    field[:, lanes_of(WINDOW + 1)] = edge
    for part, state in enumerate(in_order(odd, state_refs, slice(0, ROWS))):
        field[:, lanes_of(1 + part * BLOCKS, BLOCKS)] = jnp.where(inside, state, 0.0)


def fill_tables(odd, mesh_refs, places, coefs):
    lane = lax.broadcasted_iota(jnp.int32, (8, CELLS_DEV), 1) % LANES
    for part, mesh in enumerate(in_order(odd, mesh_refs, slice(DOF, DOF + 13))):
        cells = lanes_of(1 + part * BLOCKS, BLOCKS)
        for e in range(3):
            offset = mesh[e : e + 1, :].astype(jnp.int32)
            target = jnp.broadcast_to(offset, (8, CELLS_DEV)) + lane
            within = (target >= 0) & (target < LANES)
            places[e, :, cells] = (target & (LANES - 1)) + jnp.where(within, 0, LANES)
        for row in range(10):
            coefs[row, :, cells] = jnp.broadcast_to(mesh[3 + row : 4 + row, :], (8, CELLS_DEV))


def block_rate(source, block, places, coefs, stencil, low_half):
    here = lanes_of(block)
    centre = []
    around = []
    for r in range(3):
        rows = slice(8 * r, 8 * r + 8)
        centre.append(source[rows, here])
        around.append(
            jnp.where(low_half, source[rows, lanes_of(block + 1)], source[rows, lanes_of(block - 1)])
        )
    sums = [[None] * 3 for _ in range(3)]
    for e in range(3):
        place = places[e, :, here]
        index = place & (LANES - 1)
        within = place < LANES
        found = [lane_gather(piece, index) for piece in centre + around]
        for r in range(3):
            difference = jnp.where(within, found[r], found[3 + r]) - centre[r]
            for a in range(3):
                term = coefs[3 * a + e, :, here] * difference
                sums[a][r] = term if e == 0 else sums[a][r] + term
    turned = [coefs[9, :, here] * piece for piece in centre]
    stacked = jnp.concatenate(sums[0] + sums[1] + turned + [jnp.zeros((8, LANES), f32)], axis=0)
    high, low = two_terms(stacked)
    mixed = jnp.dot(
        stencil, jnp.concatenate([high, low, high], axis=0), preferred_element_type=f32
    )
    return mixed + jnp.concatenate(sums[2], axis=0)


def march(field, middle, places, coefs, stencil_ref):
    low_half = lax.broadcasted_iota(jnp.int32, (8, LANES), 1) < HALF
    edge = jnp.zeros((ROWS, LANES), f32)
    middle[:, lanes_of(0)] = edge
    middle[:, lanes_of(WINDOW + 1)] = edge

    stencil = stencil_ref[...]
    for index in range(PHASE_STEPS):
        for b in range(1 + index, 1 + WINDOW - index):
            rate = block_rate(field, b, places, coefs, stencil, low_half)
            middle[:, lanes_of(b)] = field[:, lanes_of(b)] + rate
        for b in range(2 + index, WINDOW - index):
            rate = block_rate(middle, b, places, coefs, stencil, low_half)
            here = lanes_of(b)
            field[:, here] = 0.5 * (field[:, here] + middle[:, here] + rate)


def pack_kernel(*refs):
    sources, out, buffers, done = refs[:6], refs[6], refs[7:13], refs[13]
    copies = [
        pltpu.make_async_copy(source, buffer, done.at[i])
        for i, (source, buffer) in enumerate(zip(sources, buffers))
    ]
    for copy in copies:
        copy.start()
    row = 0
    for copy, buffer in zip(copies, buffers):
        copy.wait()
        if len(buffer.shape) == 3:
            for d in range(DOF):
                out[d : d + 1, :] = buffer[d]
            row = DOF
        else:
            count = buffer.shape[0]
            out[row : row + count, :] = buffer[...].astype(f32)
            row += count


def first_phase_kernel(
    where_ref, first, centre, second, stencil_ref, out, places, coefs, field, middle
):
    odd = where_ref[2] % 2 == 1
    packs = (first, centre, second)
    fill_tables(odd, packs, places, coefs)
    fill_field(odd, packs, field)
    march(field, middle, places, coefs, stencil_ref)
    out[...] = field[:, lanes_of(1 + BLOCKS, BLOCKS)]


def restricted(values, index_row, restrict_matrix):
    members = (
        lax.broadcasted_iota(jnp.int32, (COARSE_DEV, CELLS_DEV), 0) == index_row
    ).astype(f32).astype(bf16)
    contract = (((1,), (1,)), ((), ()))
    totals = jnp.zeros((ROWS, COARSE_DEV), f32)
    for term in two_terms(values):
        totals = totals + lax.dot_general(term, members, contract, preferred_element_type=f32)
    counts = lax.dot_general(
        jnp.ones((16, CELLS_DEV), bf16), members, contract, preferred_element_type=f32
    )[0:1]
    result = jnp.zeros((CDOF, COARSE_DEV), f32)
    for d in range(DOF):
        result = result + restrict_matrix[:, d : d + 1] * totals[d : d + 1, :]
    result = result / counts
    return jnp.concatenate([result[i : i + 1, :] for i in range(CDOF)], axis=1)


def start_kernel(pack_ref, index_ref, matrix_ref, out):
    inside = lax.broadcasted_iota(jnp.int32, (ROWS, CELLS_DEV), 0) < DOF
    start = jnp.where(inside, pack_ref[0:ROWS, :], 0.0)
    out[...] = restricted(start, index_ref[...], matrix_ref[...])


def second_phase_kernel(
    where_ref, first, centre, second, places, coefs, stencil_ref, index_ref, matrix_ref, start_ref,
    out, message, field, middle,
):
    fill_field(where_ref[2] % 2 == 1, (first, centre, second), field)
    march(field, middle, places, coefs, stencil_ref)
    fine = field[:, lanes_of(1 + BLOCKS, BLOCKS)]
    out[...] = fine
    rows = jnp.concatenate(
        [restricted(fine, index_ref[...], matrix_ref[...]), start_ref[...]], axis=0
    )
    for copy in range(GROUP * PARTS):
        message[copy] = rows


def flipped(tiles, even_row):
    up = pltpu.roll(jnp.concatenate([tiles[1:], tiles[:1]], axis=0), 7, axis=1)
    down = pltpu.roll(jnp.concatenate([tiles[7:], tiles[:7]], axis=0), 1, axis=1)
    return jnp.where(even_row, up, down)


def compose_kernel(inverse_ref, out, out_twice):
    shape = (8, 8, LANES)
    row = lax.broadcasted_iota(jnp.int32, shape, 1)
    lane = lax.broadcasted_iota(jnp.int32, shape, 2)
    turn = lax.broadcasted_iota(jnp.int32, shape, 0)
    even_row = row % 2 == 0
    first_lane = lane == 0
    last_lane = lane == LANES - 1
    own = 1.0 - 2.0 * coupling - opposite
    blocks = []
    for by in range(CDOF):
        pieces = []
        for i in range(CDOF):
            j = (i - by) % CDOF
            for h in range(2):
                pieces.append(inverse_ref[i, j : j + 1, lanes_of(h)])
        blocks.append(jnp.concatenate(pieces, axis=0)[None])
    reach = {0: jnp.where(turn == 0, 1.0, 0.0)}
    for repeat in range(2 * COARSE_STEPS):
        swapped = {o: flipped(tiles, even_row) for o, tiles in reach.items()}
        blended = {}
        for o in range(-repeat - 1, repeat + 2):
            total = jnp.zeros(shape, f32)
            if o in reach:
                total = own * reach[o] + opposite * swapped[o]
            if o - 1 in reach:
                edge = jnp.where(last_lane, swapped[o - 1], reach[o - 1])
                total = total + coupling * pltpu.roll(edge, 1, axis=2)
            if o + 1 in reach:
                edge = jnp.where(first_lane, swapped[o + 1], reach[o + 1])
                total = total + coupling * pltpu.roll(edge, LANES - 1, axis=2)
            blended[o] = total
        reach = {}
        for o, tiles in blended.items():
            total = blocks[0] * tiles
            for by in range(1, CDOF):
                turned = jnp.concatenate([tiles[8 - 2 * by :], tiles[: 8 - 2 * by]], axis=0)
                total = total + blocks[by] * pltpu.roll(turned, 2 * by, axis=1)
            reach[o] = total
        if (repeat + 1) % COARSE_STEPS == 0:
            held = out if repeat < COARSE_STEPS else out_twice
            for o, tiles in reach.items():
                held[o + repeat + 1] = tiles if o == 0 else pltpu.roll(tiles, -o % LANES, axis=2)


def added(terms):
    while len(terms) > 1:
        terms = [sum(terms[i : i + 2][1:], terms[i]) for i in range(0, len(terms), 2)]
    return terms[0]


def coarse_slice(vector, operator_ref):
    turns = [vector] + [pltpu.roll(vector, d, axis=0) for d in range(1, 8)]
    reach = operator_ref.shape[0] // 2
    shares = []
    for o in range(-reach, reach + 1):
        share = added([operator_ref[o + reach, d] * turns[d] for d in range(8)])
        shares.append(share if o == 0 else pltpu.roll(share, o % LANES, axis=1))
    return added(shares)


def group_kernel(where_ref, gathered, operator_ref, ends_out, own_out, finish, start):
    group = where_ref[0]
    place = where_ref[1]
    quarter = lax.broadcasted_iota(jnp.int32, (GROUP, LANES), 1) // COARSE_DEV
    for kind, ref in enumerate((finish, start)):
        for i in range(CDOF):
            for h in range(2):
                held = jnp.zeros((GROUP, LANES), f32)
                for q in range(4):
                    p = 4 * h + q
                    rows = gathered[pl.ds(2 * p + kind, GROUP, stride=2 * PARTS), :]
                    by = (q - i) * COARSE_DEV % LANES
                    moved = rows if by == 0 else pltpu.roll(rows, by, axis=1)
                    held = jnp.where(quarter == q, moved, held)
                ref[pl.ds((2 * i + h) * GROUP, GROUP), :] = held

    def of_slice(ref, n):
        return ref[pl.ds(n, 8, stride=GROUP), :]

    chain = None
    own = jnp.zeros((8, LANES), f32)
    for n in range(GROUP):
        coarse = coarse_slice(of_slice(start, n), operator_ref)
        if n == 0:
            coarse = jnp.where(group > 0, coarse, 0.0)
        jump = of_slice(finish, n) - coarse
        chain = jump if n == 0 else coarse_slice(chain, operator_ref) + jump
        own = jnp.where(place == n, chain, own)
    for copy in range(GROUPS):
        ends_out[copy] = chain
    own_out[0] = own
    own_out[1] = finish[pl.ds(place, 8, stride=GROUP), :]


def correct_kernel(
    where_ref, ends, own_ref, operator_ref, twice_ref, fine_ref, index_ref, matrix_ref, out
):
    group = where_ref[0]
    place = where_ref[1]
    part = where_ref[2]

    def advance(count, vector, ref):
        return lax.fori_loop(0, count, lambda n, now: coarse_slice(now, ref), vector)

    def link(k, vector):
        return advance(GROUP // 2, vector, twice_ref) + ends[k]

    before = lax.fori_loop(1, group, link, ends[0])
    count = jnp.where(group > 0, place + 1, 0)
    before = advance(count % 2, advance(count // 2, before, twice_ref), operator_ref)
    chain = own_ref[0] + jnp.where(group > 0, before, 0.0)
    change = chain - own_ref[1]
    upper = part >= PARTS // 2
    spread = jnp.zeros((ROWS, LANES), f32)
    for i in range(CDOF):
        chosen = jnp.where(upper, change[2 * i + 1 : 2 * i + 2], change[2 * i : 2 * i + 1])
        spread = spread + matrix_ref[:, i : i + 1] * jnp.broadcast_to(chosen, (ROWS, LANES))
    members = (
        lax.broadcasted_iota(jnp.int32, (LANES, CELLS_DEV), 0)
        == index_ref[...] + COARSE_DEV * (part % 4)
    ).astype(f32).astype(bf16)
    total = fine_ref[...]
    for term in two_terms(spread):
        total = total + jnp.dot(term, members, preferred_element_type=f32)
    for d in range(DOF):
        out[d] = total[d : d + 1, :]


TABLE = (WINDOW + 2) * LANES
march_scratch = [pltpu.VMEM((ROWS, TABLE), f32)] * 2


PACK_BYTES = 63 * 1024 * 1024 + 896 * 1024
params = pltpu.CompilerParams(vmem_limit_bytes=32 * 1024 * 1024)


def both_sides(values):
    pairs = [(i, i ^ 1) for i in range(PARTS)]
    others = [(i, (((i + 1) ^ 1) - 1) % PARTS) for i in range(PARTS)]
    return lax.ppermute(values, "space", pairs), lax.ppermute(values, "space", others)


smem = pl.BlockSpec(memory_space=pltpu.SMEM)


def local(
    states,
    neighbour,
    edge_x,
    edge_y,
    edge_damp,
    coriolis,
    flux_x,
    flux_y,
    rotation,
    restrict_matrix,
    prolong_matrix,
    restrict_index,
    coarse_inverse,
):
    parts = (
        states.transpose(1, 0, 2), neighbour, edge_x, edge_y, edge_damp, coriolis[None, :]
    )
    pack = pl.pallas_call(
        pack_kernel,
        out_shape=jax.ShapeDtypeStruct((DOF + 13, CELLS_DEV), f32),
        in_specs=[pl.BlockSpec(memory_space=pltpu.HBM)] * len(parts),
        out_specs=vmem,
        scratch_shapes=[pltpu.VMEM(part.shape, part.dtype) for part in parts]
        + [pltpu.SemaphoreType.DMA((len(parts),))],
        compiler_params=pltpu.CompilerParams(vmem_limit_bytes=PACK_BYTES),
    )(*parts)
    first, second = both_sides(pack)
    slice_here = lax.axis_index("tm")
    where = jnp.stack([slice_here // GROUP, slice_here % GROUP, lax.axis_index("space")])
    where = where.astype(jnp.int32)
    wide = [jnp.pad(m, ((0, ROWS - DOF), (0, ROWS - DOF))) for m in (flux_x, flux_y, rotation)]
    stencil = jnp.concatenate(wide + [jnp.zeros((ROWS, 8), f32)], axis=1)
    high = stencil.astype(bf16)
    low = (stencil - lax.reduce_precision(stencil, 8, 7)).astype(bf16)
    stencil_terms = jnp.concatenate([high, high, low], axis=1)
    index_row = restrict_index[None, :]
    start = pl.pallas_call(
        start_kernel,
        out_shape=jax.ShapeDtypeStruct((1, LANES), f32),
        in_specs=[vmem] * 3,
        out_specs=vmem,
        compiler_params=params,
        cost_estimate=pl.CostEstimate(flops=4000000, bytes_accessed=200000, transcendentals=0),
    )(pack, index_row, restrict_matrix)

    half, places, coefs = pl.pallas_call(
        first_phase_kernel,
        out_shape=(
            jax.ShapeDtypeStruct((ROWS, CELLS_DEV), f32),
            jax.ShapeDtypeStruct((3, 8, TABLE), jnp.int32),
            jax.ShapeDtypeStruct((10, 8, TABLE), f32),
        ),
        in_specs=[smem] + [vmem] * 4,
        out_specs=(vmem, vmem, vmem),
        scratch_shapes=march_scratch,
        compiler_params=params,
    )(where, first, pack, second, stencil_terms)
    late_inverse, half = lax.optimization_barrier((coarse_inverse, half))
    half_first, half_second = both_sides(half)
    operator, operator_twice = pl.pallas_call(
        compose_kernel,
        out_shape=tuple(
            jax.ShapeDtypeStruct((2 * reach + 1, 8, 8, LANES), f32)
            for reach in (COARSE_STEPS, 2 * COARSE_STEPS)
        ),
        in_specs=[vmem],
        out_specs=(vmem, vmem),
        compiler_params=params,
        cost_estimate=pl.CostEstimate(flops=12000000, bytes_accessed=900000, transcendentals=0),
    )(late_inverse)
    fine, message = pl.pallas_call(
        second_phase_kernel,
        out_shape=(
            jax.ShapeDtypeStruct((ROWS, CELLS_DEV), f32),
            jax.ShapeDtypeStruct((GROUP * PARTS, 2, LANES), f32),
        ),
        in_specs=[smem] + [vmem] * 9,
        out_specs=(vmem, vmem),
        scratch_shapes=march_scratch,
        compiler_params=params,
    )(
        where, half_first, half, half_second, places, coefs, stencil_terms, index_row,
        restrict_matrix, start,
    )

    spread_matrix = jnp.pad(prolong_matrix, ((0, ROWS - DOF), (0, 0)))
    message, operator, operator_twice, spread_matrix, where, index_row = lax.optimization_barrier(
        (message, operator, operator_twice, spread_matrix, where, index_row)
    )
    axes = ("tm", "space")
    members = GROUP * PARTS
    inside = [[g * members + m for m in range(members)] for g in range(GROUPS)]
    across = [[g * members + m for g in range(GROUPS)] for m in range(members)]
    gathered = lax.all_to_all(message, axes, 0, 0, tiled=True, axis_index_groups=inside)
    ends, own = pl.pallas_call(
        group_kernel,
        out_shape=(
            jax.ShapeDtypeStruct((GROUPS, 8, LANES), f32),
            jax.ShapeDtypeStruct((2, 8, LANES), f32),
        ),
        in_specs=[smem, vmem, vmem],
        out_specs=(vmem, vmem),
        scratch_shapes=[pltpu.VMEM((8 * GROUP, LANES), f32)] * 2,
        compiler_params=params,
    )(where, gathered.reshape(GROUP * PARTS * 2, LANES), operator)
    ends = lax.all_to_all(ends, axes, 0, 0, tiled=True, axis_index_groups=across)
    updated = pl.pallas_call(
        correct_kernel,
        out_shape=jax.ShapeDtypeStruct((DOF, 1, CELLS_DEV), f32),
        in_specs=[smem] + [vmem] * 7,
        out_specs=vmem,
        compiler_params=params,
    )(where, ends, own, operator, operator_twice, fine, index_row, spread_matrix)
    return updated.transpose(1, 0, 2)


def solution(mesh):
    in_specs = (
        P("tm", None, "space"),
        P(None, "space"),
        P(None, "space"),
        P(None, "space"),
        P(None, "space"),
        P("space"),
        P(),
        P(),
        P(),
        P(),
        P(),
        P("space"),
        P(),
    )
    out_specs = P("tm", None, "space")
    return jax.shard_map(local, mesh=mesh, in_specs=in_specs, out_specs=out_specs, check_vma=False)
```

```python
import functools

import jax
import jax.numpy as jnp
from jax import lax
from jax.experimental import pallas as pl
from jax.experimental.pallas import tpu as pltpu
from jax.sharding import PartitionSpec as P

DOF = 21
CDOF = 4
ROWS = 24
LANES = 128
HALF = 64
CELLS_DEV = 1024
COARSE_DEV = 32
COARSE_STEPS = 4
PARTS = 8
SLICES = 64
GROUP = 8
GROUPS = SLICES // GROUP
BLOCKS = CELLS_DEV // LANES
PHASE_STEPS = 8
WINDOW = 3 * BLOCKS
MESH_END = DOF + 13

coupling = 0.1
opposite = 0.25
highest = lax.Precision.HIGHEST
f32 = jnp.float32
bf16 = jnp.bfloat16
vmem = pl.BlockSpec(memory_space=pltpu.VMEM)


def lane_gather(values, index):
    numbers = lax.GatherDimensionNumbers(
        offset_dims=(),
        collapsed_slice_dims=(1,),
        start_index_map=(1,),
        operand_batching_dims=(0,),
        start_indices_batching_dims=(0,),
    )
    return lax.gather(
        values, index[..., None], numbers, (1, 1), mode=lax.GatherScatterMode.PROMISE_IN_BOUNDS
    )


def two_terms(values):
    high = values.astype(bf16)
    return high, (values - high.astype(f32)).astype(bf16)


def lanes_of(block, count=1):
    return slice(block * LANES, (block + count) * LANES)


def sides(odd, first, second, rows):
    one, two = first[rows, :], second[rows, :]
    return jnp.where(odd, one, two), jnp.where(odd, two, one)


def in_order(odd, refs, rows):
    left, right = sides(odd, refs[0], refs[2], rows)
    return left, refs[1][rows, :], right


def fill_field(odd, state_refs, field):
    inside = lax.broadcasted_iota(jnp.int32, (ROWS, CELLS_DEV), 0) < DOF
    edge = jnp.zeros((ROWS, LANES), f32)
    field[:, lanes_of(0)] = edge
    field[:, lanes_of(WINDOW + 1)] = edge
    for part, state in enumerate(in_order(odd, state_refs, slice(0, ROWS))):
        field[:, lanes_of(1 + part * BLOCKS, BLOCKS)] = jnp.where(inside, state, 0.0)


def fill_tables(odd, mesh_refs, places, coefs):
    lane = lax.broadcasted_iota(jnp.int32, (8, CELLS_DEV), 1) % LANES
    for part, mesh in enumerate(in_order(odd, mesh_refs, slice(DOF, MESH_END))):
        cells = lanes_of(1 + part * BLOCKS, BLOCKS)
        for e in range(3):
            offset = mesh[e : e + 1, :].astype(jnp.int32)
            target = jnp.broadcast_to(offset, (8, CELLS_DEV)) + lane
            within = (target >= 0) & (target < LANES)
            places[e, :, cells] = (target & (LANES - 1)) + jnp.where(within, 0, LANES)
        for row in range(10):
            coefs[row, :, cells] = jnp.broadcast_to(mesh[3 + row : 4 + row, :], (8, CELLS_DEV))


def block_rate(source, block, places, coefs, stencil, low_half):
    here = lanes_of(block)
    centre = []
    around = []
    for r in range(3):
        rows = slice(8 * r, 8 * r + 8)
        centre.append(source[rows, here])
        around.append(
            jnp.where(low_half, source[rows, lanes_of(block + 1)], source[rows, lanes_of(block - 1)])
        )
    sums = [[None] * 3 for _ in range(3)]
    for e in range(3):
        place = places[e, :, here]
        index = place & (LANES - 1)
        within = place < LANES
        found = [lane_gather(piece, index) for piece in centre + around]
        for r in range(3):
            difference = jnp.where(within, found[r], found[3 + r]) - centre[r]
            for a in range(3):
                term = coefs[3 * a + e, :, here] * difference
                sums[a][r] = term if e == 0 else sums[a][r] + term
    turned = [coefs[9, :, here] * piece for piece in centre]
    stacked = jnp.concatenate(sums[0] + sums[1] + turned + [jnp.zeros((8, LANES), f32)], axis=0)
    high, low = two_terms(stacked)
    mixed = jnp.dot(
        stencil, jnp.concatenate([high, low, high], axis=0), preferred_element_type=f32
    )
    return mixed + jnp.concatenate(sums[2], axis=0)


def march(field, middle, places, coefs, stencil_ref):
    low_half = lax.broadcasted_iota(jnp.int32, (8, LANES), 1) < HALF
    edge = jnp.zeros((ROWS, LANES), f32)
    middle[:, lanes_of(0)] = edge
    middle[:, lanes_of(WINDOW + 1)] = edge

    stencil = stencil_ref[...]
    for index in range(PHASE_STEPS):
        for b in range(1 + index, 1 + WINDOW - index):
            rate = block_rate(field, b, places, coefs, stencil, low_half)
            middle[:, lanes_of(b)] = field[:, lanes_of(b)] + rate
        for b in range(2 + index, WINDOW - index):
            rate = block_rate(middle, b, places, coefs, stencil, low_half)
            here = lanes_of(b)
            field[:, here] = 0.5 * (field[:, here] + middle[:, here] + rate)


def pack_kernel(*refs):
    sources, out, buffers, done = refs[:7], refs[7], refs[8:15], refs[15]
    copies = [
        pltpu.make_async_copy(source, buffer, done.at[i])
        for i, (source, buffer) in enumerate(zip(sources, buffers))
    ]
    for copy in copies:
        copy.start()
    row = 0
    for copy, buffer in zip(copies, buffers):
        copy.wait()
        if len(buffer.shape) == 3:
            for d in range(DOF):
                out[d : d + 1, :] = buffer[d]
            row = DOF
        else:
            count = buffer.shape[0]
            out[row : row + count, :] = buffer[...].astype(f32)
            row += count


def restricted(values, members, restrict_matrix):
    contract = (((1,), (1,)), ((), ()))
    totals = jnp.zeros((ROWS, COARSE_DEV), f32)
    for term in two_terms(values):
        totals = totals + lax.dot_general(term, members, contract, preferred_element_type=f32)
    counts = lax.dot_general(
        jnp.ones((16, CELLS_DEV), bf16), members, contract, preferred_element_type=f32
    )[0:1]
    result = jnp.zeros((CDOF, COARSE_DEV), f32)
    for d in range(DOF):
        result = result + restrict_matrix[0:CDOF, d : d + 1] * totals[d : d + 1, :]
    result = result / counts
    return jnp.concatenate([result[i : i + 1, :] for i in range(CDOF)], axis=1)


def first_phase_kernel(
    where_ref, first, centre, second, stencil_ref, matrix_ref,
    out, places, coefs, start_out, members_out, field, middle,
):
    odd = where_ref[2] % 2 == 1
    packs = (first, centre, second)
    fill_tables(odd, packs, places, coefs)
    fill_field(odd, packs, field)
    start = field[:, lanes_of(1 + BLOCKS, BLOCKS)]
    index_row = centre[MESH_END : MESH_END + 1, :].astype(jnp.int32)
    members = (
        lax.broadcasted_iota(jnp.int32, (COARSE_DEV, CELLS_DEV), 0) == index_row
    ).astype(f32).astype(bf16)
    members_out[...] = members
    start_out[...] = restricted(start, members, matrix_ref[...])
    march(field, middle, places, coefs, stencil_ref)
    out[...] = field[:, lanes_of(1 + BLOCKS, BLOCKS)]


def second_phase_kernel(
    where_ref, first, centre, second, places, coefs, stencil_ref, members_ref, matrix_ref, start_ref,
    out, message, field, middle,
):
    fill_field(where_ref[2] % 2 == 1, (first, centre, second), field)
    march(field, middle, places, coefs, stencil_ref)
    fine = field[:, lanes_of(1 + BLOCKS, BLOCKS)]
    out[...] = fine
    rows = jnp.concatenate(
        [restricted(fine, members_ref[...], matrix_ref[...]), start_ref[...]], axis=0
    )
    for copy in range(GROUP * PARTS):
        message[copy] = rows


def flipped(tiles, even_row):
    up = pltpu.roll(jnp.concatenate([tiles[1:], tiles[:1]], axis=0), 7, axis=1)
    down = pltpu.roll(jnp.concatenate([tiles[7:], tiles[:7]], axis=0), 1, axis=1)
    return jnp.where(even_row, up, down)


def compose_kernel(inverse_ref, out, out_twice):
    shape = (8, 8, LANES)
    row = lax.broadcasted_iota(jnp.int32, shape, 1)
    lane = lax.broadcasted_iota(jnp.int32, shape, 2)
    turn = lax.broadcasted_iota(jnp.int32, shape, 0)
    even_row = row % 2 == 0
    first_lane = lane == 0
    last_lane = lane == LANES - 1
    own = 1.0 - 2.0 * coupling - opposite
    blocks = []
    for by in range(CDOF):
        pieces = []
        for i in range(CDOF):
            j = (i - by) % CDOF
            for h in range(2):
                pieces.append(inverse_ref[i, j : j + 1, lanes_of(h)])
        blocks.append(jnp.concatenate(pieces, axis=0)[None])
    reach = {0: jnp.where(turn == 0, 1.0, 0.0)}
    for repeat in range(2 * COARSE_STEPS):
        swapped = {o: flipped(tiles, even_row) for o, tiles in reach.items()}
        blended = {}
        for o in range(-repeat - 1, repeat + 2):
            total = jnp.zeros(shape, f32)
            if o in reach:
                total = own * reach[o] + opposite * swapped[o]
            if o - 1 in reach:
                edge = jnp.where(last_lane, swapped[o - 1], reach[o - 1])
                total = total + coupling * pltpu.roll(edge, 1, axis=2)
            if o + 1 in reach:
                edge = jnp.where(first_lane, swapped[o + 1], reach[o + 1])
                total = total + coupling * pltpu.roll(edge, LANES - 1, axis=2)
            blended[o] = total
        reach = {}
        for o, tiles in blended.items():
            total = blocks[0] * tiles
            for by in range(1, CDOF):
                turned = jnp.concatenate([tiles[8 - 2 * by :], tiles[: 8 - 2 * by]], axis=0)
                total = total + blocks[by] * pltpu.roll(turned, 2 * by, axis=1)
            reach[o] = total
        if (repeat + 1) % COARSE_STEPS == 0:
            held = out if repeat < COARSE_STEPS else out_twice
            for o, tiles in reach.items():
                held[o + repeat + 1] = tiles if o == 0 else pltpu.roll(tiles, -o % LANES, axis=2)


def added(terms):
    while len(terms) > 1:
        terms = [sum(terms[i : i + 2][1:], terms[i]) for i in range(0, len(terms), 2)]
    return terms[0]


def coarse_slice(vector, operator_ref):
    turns = [vector] + [pltpu.roll(vector, d, axis=0) for d in range(1, 8)]
    reach = operator_ref.shape[0] // 2
    shares = []
    for o in range(-reach, reach + 1):
        share = added([operator_ref[o + reach, d] * turns[d] for d in range(8)])
        shares.append(share if o == 0 else pltpu.roll(share, o % LANES, axis=1))
    return added(shares)


def group_kernel(where_ref, gathered, operator_ref, ends_out, own_out, finish, start):
    group = where_ref[0]
    place = where_ref[1]
    quarter = lax.broadcasted_iota(jnp.int32, (GROUP, LANES), 1) // COARSE_DEV
    for kind, ref in enumerate((finish, start)):
        for i in range(CDOF):
            for h in range(2):
                held = jnp.zeros((GROUP, LANES), f32)
                for q in range(4):
                    p = 4 * h + q
                    rows = gathered[pl.ds(2 * p + kind, GROUP, stride=2 * PARTS), :]
                    by = (q - i) * COARSE_DEV % LANES
                    moved = rows if by == 0 else pltpu.roll(rows, by, axis=1)
                    held = jnp.where(quarter == q, moved, held)
                ref[pl.ds((2 * i + h) * GROUP, GROUP), :] = held

    def of_slice(ref, n):
        return ref[pl.ds(n, 8, stride=GROUP), :]

    chain = None
    own = jnp.zeros((8, LANES), f32)
    for n in range(GROUP):
        coarse = coarse_slice(of_slice(start, n), operator_ref)
        if n == 0:
            coarse = jnp.where(group > 0, coarse, 0.0)
        jump = of_slice(finish, n) - coarse
        chain = jump if n == 0 else coarse_slice(chain, operator_ref) + jump
        own = jnp.where(place == n, chain, own)
    for copy in range(GROUPS):
        ends_out[copy] = chain
    own_out[0] = own
    own_out[1] = finish[pl.ds(place, 8, stride=GROUP), :]


def correct_kernel(
    where_ref, ends, own_ref, operator_ref, twice_ref, fine_ref, members_ref, matrix_ref, out
):
    group = where_ref[0]
    place = where_ref[1]
    part = where_ref[2]

    def advance(count, vector, ref):
        return lax.fori_loop(0, count, lambda n, now: coarse_slice(now, ref), vector)

    def link(k, vector):
        return advance(GROUP // 2, vector, twice_ref) + ends[k]

    before = lax.fori_loop(1, group, link, ends[0])
    count = jnp.where(group > 0, place + 1, 0)
    before = advance(count % 2, advance(count // 2, before, twice_ref), operator_ref)
    chain = own_ref[0] + jnp.where(group > 0, before, 0.0)
    change = chain - own_ref[1]
    upper = part >= PARTS // 2
    spread = jnp.zeros((ROWS, LANES), f32)
    for i in range(CDOF):
        chosen = jnp.where(upper, change[2 * i + 1 : 2 * i + 2], change[2 * i : 2 * i + 1])
        spread = spread + matrix_ref[:, i : i + 1] * jnp.broadcast_to(chosen, (ROWS, LANES))
    spread = pltpu.roll(spread, (4 - part % 4) * COARSE_DEV % LANES, axis=1)[:, 0:COARSE_DEV]
    total = fine_ref[...]
    for term in two_terms(spread):
        total = total + jnp.dot(term, members_ref[...], preferred_element_type=f32)
    for d in range(DOF):
        out[d] = total[d : d + 1, :]


TABLE = (WINDOW + 2) * LANES
march_scratch = [pltpu.VMEM((ROWS, TABLE), f32)] * 2


params = pltpu.CompilerParams(vmem_limit_bytes=32 * 1024 * 1024)


def both_sides(values):
    pairs = [(i, i ^ 1) for i in range(PARTS)]
    others = [(i, (((i + 1) ^ 1) - 1) % PARTS) for i in range(PARTS)]
    return lax.ppermute(values, "space", pairs), lax.ppermute(values, "space", others)


smem = pl.BlockSpec(memory_space=pltpu.SMEM)


def local(
    states,
    neighbour,
    edge_x,
    edge_y,
    edge_damp,
    coriolis,
    flux_x,
    flux_y,
    rotation,
    restrict_matrix,
    prolong_matrix,
    restrict_index,
    coarse_inverse,
):
    parts = (
        states.transpose(1, 0, 2),
        neighbour,
        edge_x,
        edge_y,
        edge_damp,
        coriolis[None, :],
        restrict_index[None, :],
    )
    pack = pl.pallas_call(
        pack_kernel,
        out_shape=jax.ShapeDtypeStruct((MESH_END + 1, CELLS_DEV), f32),
        in_specs=[pl.BlockSpec(memory_space=pltpu.HBM)] * len(parts),
        out_specs=vmem,
        scratch_shapes=[pltpu.VMEM(part.shape, part.dtype) for part in parts]
        + [pltpu.SemaphoreType.DMA((len(parts),))],
        compiler_params=params,
    )(*[pltpu.with_memory_space_constraint(part, pltpu.HBM) for part in parts])
    first, second = both_sides(pack)
    slice_here = lax.axis_index("tm")
    where = jnp.stack([slice_here // GROUP, slice_here % GROUP, lax.axis_index("space")])
    where = where.astype(jnp.int32)
    wide = [jnp.pad(m, ((0, ROWS - DOF), (0, ROWS - DOF))) for m in (flux_x, flux_y, rotation)]
    stencil = jnp.concatenate(wide + [jnp.zeros((ROWS, 8), f32)], axis=1)
    high = stencil.astype(bf16)
    low = (stencil - lax.reduce_precision(stencil, 8, 7)).astype(bf16)
    stencil_terms = jnp.concatenate([high, high, low], axis=1)
    means_matrix = jnp.pad(restrict_matrix, ((0, 4), (0, LANES - DOF)))
    half, places, coefs, start, members = pl.pallas_call(
        first_phase_kernel,
        out_shape=(
            jax.ShapeDtypeStruct((ROWS, CELLS_DEV), f32),
            jax.ShapeDtypeStruct((3, 8, TABLE), jnp.int32),
            jax.ShapeDtypeStruct((10, 8, TABLE), f32),
            jax.ShapeDtypeStruct((1, LANES), f32),
            jax.ShapeDtypeStruct((COARSE_DEV, CELLS_DEV), bf16),
        ),
        in_specs=[smem] + [vmem] * 5,
        out_specs=(vmem,) * 5,
        scratch_shapes=march_scratch,
        compiler_params=params,
    )(where, first, pack, second, stencil_terms, means_matrix)
    half_first, half_second = both_sides(half)
    fine, message = pl.pallas_call(
        second_phase_kernel,
        out_shape=(
            jax.ShapeDtypeStruct((ROWS, CELLS_DEV), f32),
            jax.ShapeDtypeStruct((GROUP * PARTS, 2, LANES), f32),
        ),
        in_specs=[smem] + [vmem] * 9,
        out_specs=(vmem, vmem),
        scratch_shapes=march_scratch,
        compiler_params=params,
    )(
        where, half_first, half, half_second, places, coefs, stencil_terms, members,
        means_matrix, start,
    )

    late_inverse, late_prolong, message = lax.optimization_barrier(
        (coarse_inverse, prolong_matrix, message)
    )
    operator, operator_twice = pl.pallas_call(
        compose_kernel,
        out_shape=tuple(
            jax.ShapeDtypeStruct((2 * reach + 1, 8, 8, LANES), f32)
            for reach in (COARSE_STEPS, 2 * COARSE_STEPS)
        ),
        in_specs=[vmem],
        out_specs=(vmem, vmem),
        compiler_params=params,
        cost_estimate=pl.CostEstimate(flops=12000000, bytes_accessed=900000, transcendentals=0),
    )(late_inverse)
    spread_matrix = jnp.pad(late_prolong, ((0, ROWS - DOF), (0, 0)))
    axes = ("tm", "space")
    count = GROUP * PARTS
    inside = [[g * count + m for m in range(count)] for g in range(GROUPS)]
    across = [[g * count + m for g in range(GROUPS)] for m in range(count)]
    gathered = lax.all_to_all(message, axes, 0, 0, tiled=True, axis_index_groups=inside)
    ends, own = pl.pallas_call(
        group_kernel,
        out_shape=(
            jax.ShapeDtypeStruct((GROUPS, 8, LANES), f32),
            jax.ShapeDtypeStruct((2, 8, LANES), f32),
        ),
        in_specs=[smem, vmem, vmem],
        out_specs=(vmem, vmem),
        scratch_shapes=[pltpu.VMEM((8 * GROUP, LANES), f32)] * 2,
        compiler_params=params,
    )(where, gathered.reshape(GROUP * PARTS * 2, LANES), operator)
    ends, spread_matrix = lax.optimization_barrier((ends, spread_matrix))
    ends = lax.all_to_all(ends, axes, 0, 0, tiled=True, axis_index_groups=across)
    updated = pl.pallas_call(
        correct_kernel,
        out_shape=jax.ShapeDtypeStruct((DOF, 1, CELLS_DEV), f32),
        in_specs=[smem] + [vmem] * 7,
        out_specs=vmem,
        compiler_params=params,
    )(where, ends, own, operator, operator_twice, fine, members, spread_matrix)
    return updated.transpose(1, 0, 2)


def solution(mesh):
    in_specs = (
        P("tm", None, "space"),
        P(None, "space"),
        P(None, "space"),
        P(None, "space"),
        P(None, "space"),
        P("space"),
        P(),
        P(),
        P(),
        P(),
        P(),
        P("space"),
        P(),
    )
    out_specs = P("tm", None, "space")
    return jax.shard_map(local, mesh=mesh, in_specs=in_specs, out_specs=out_specs, check_vma=False)
```

```python
import functools

import jax
import jax.numpy as jnp
from jax import lax
from jax.experimental import pallas as pl
from jax.experimental.pallas import tpu as pltpu
from jax.sharding import PartitionSpec as P

DOF = 21
CDOF = 4
ROWS = 24
LANES = 128
HALF = 64
CELLS_DEV = 1024
COARSE_DEV = 32
COARSE_STEPS = 4
PARTS = 8
SLICES = 64
GROUP = 8
GROUPS = SLICES // GROUP
BLOCKS = CELLS_DEV // LANES
PHASE_STEPS = 8
WINDOW = 3 * BLOCKS
MESH_END = DOF + 13

coupling = 0.1
opposite = 0.25
highest = lax.Precision.HIGHEST
f32 = jnp.float32
bf16 = jnp.bfloat16
vmem = pl.BlockSpec(memory_space=pltpu.VMEM)


def lane_gather(values, index):
    numbers = lax.GatherDimensionNumbers(
        offset_dims=(),
        collapsed_slice_dims=(1,),
        start_index_map=(1,),
        operand_batching_dims=(0,),
        start_indices_batching_dims=(0,),
    )
    return lax.gather(
        values, index[..., None], numbers, (1, 1), mode=lax.GatherScatterMode.PROMISE_IN_BOUNDS
    )


def two_terms(values):
    high = values.astype(bf16)
    return high, (values - high.astype(f32)).astype(bf16)


def lanes_of(block, count=1):
    return slice(block * LANES, (block + count) * LANES)


def sides(odd, first, second, rows):
    one, two = first[rows, :], second[rows, :]
    return jnp.where(odd, one, two), jnp.where(odd, two, one)


def in_order(odd, refs, rows):
    left, right = sides(odd, refs[0], refs[2], rows)
    return left, refs[1][rows, :], right


def fill_field(odd, state_refs, field):
    inside = lax.broadcasted_iota(jnp.int32, (ROWS, CELLS_DEV), 0) < DOF
    edge = jnp.zeros((ROWS, LANES), f32)
    field[:, lanes_of(0)] = edge
    field[:, lanes_of(WINDOW + 1)] = edge
    for part, state in enumerate(in_order(odd, state_refs, slice(0, ROWS))):
        field[:, lanes_of(1 + part * BLOCKS, BLOCKS)] = jnp.where(inside, state, 0.0)


def fill_tables(odd, mesh_refs, places, coefs):
    lane = lax.broadcasted_iota(jnp.int32, (8, CELLS_DEV), 1) % LANES
    for part, mesh in enumerate(in_order(odd, mesh_refs, slice(DOF, MESH_END))):
        cells = lanes_of(1 + part * BLOCKS, BLOCKS)
        for e in range(3):
            offset = mesh[e : e + 1, :].astype(jnp.int32)
            target = jnp.broadcast_to(offset, (8, CELLS_DEV)) + lane
            within = (target >= 0) & (target < LANES)
            places[e, :, cells] = (target & (LANES - 1)) + jnp.where(within, 0, LANES)
        for row in range(10):
            coefs[row, :, cells] = jnp.broadcast_to(mesh[3 + row : 4 + row, :], (8, CELLS_DEV))


def block_rate(source, block, places, coefs, stencil, low_half):
    here = lanes_of(block)
    centre = []
    around = []
    for r in range(3):
        rows = slice(8 * r, 8 * r + 8)
        centre.append(source[rows, here])
        around.append(
            jnp.where(low_half, source[rows, lanes_of(block + 1)], source[rows, lanes_of(block - 1)])
        )
    sums = [[None] * 3 for _ in range(3)]
    for e in range(3):
        place = places[e, :, here]
        index = place & (LANES - 1)
        within = place < LANES
        found = [lane_gather(piece, index) for piece in centre + around]
        for r in range(3):
            difference = jnp.where(within, found[r], found[3 + r]) - centre[r]
            for a in range(3):
                term = coefs[3 * a + e, :, here] * difference
                sums[a][r] = term if e == 0 else sums[a][r] + term
    turned = [coefs[9, :, here] * piece for piece in centre]
    stacked = jnp.concatenate(sums[0] + sums[1] + turned + [jnp.zeros((8, LANES), f32)], axis=0)
    high, low = two_terms(stacked)
    mixed = jnp.dot(
        stencil, jnp.concatenate([high, low, high], axis=0), preferred_element_type=f32
    )
    return mixed + jnp.concatenate(sums[2], axis=0)


def march(field, middle, places, coefs, stencil_ref):
    low_half = lax.broadcasted_iota(jnp.int32, (8, LANES), 1) < HALF
    edge = jnp.zeros((ROWS, LANES), f32)
    middle[:, lanes_of(0)] = edge
    middle[:, lanes_of(WINDOW + 1)] = edge

    stencil = stencil_ref[...]
    for index in range(PHASE_STEPS):
        for b in range(1 + index, 1 + WINDOW - index):
            rate = block_rate(field, b, places, coefs, stencil, low_half)
            middle[:, lanes_of(b)] = field[:, lanes_of(b)] + rate
        for b in range(2 + index, WINDOW - index):
            rate = block_rate(middle, b, places, coefs, stencil, low_half)
            here = lanes_of(b)
            field[:, here] = 0.5 * (field[:, here] + middle[:, here] + rate)


def pack_kernel(*refs):
    sources, out, buffers, done = refs[:7], refs[7], refs[8:15], refs[15]
    copies = [
        pltpu.make_async_copy(source, buffer, done.at[i])
        for i, (source, buffer) in enumerate(zip(sources, buffers))
    ]
    for copy in copies:
        copy.start()
    row = 0
    for copy, buffer in zip(copies, buffers):
        copy.wait()
        if len(buffer.shape) == 3:
            for d in range(DOF):
                out[d : d + 1, :] = buffer[d]
            row = DOF
        else:
            count = buffer.shape[0]
            out[row : row + count, :] = buffer[...].astype(f32)
            row += count


def added(terms):
    while len(terms) > 1:
        terms = [sum(terms[i : i + 2][1:], terms[i]) for i in range(0, len(terms), 2)]
    return terms[0]


def restricted(values, members, restrict_matrix):
    contract = (((1,), (1,)), ((), ()))
    totals = jnp.zeros((ROWS, COARSE_DEV), f32)
    for term in two_terms(values):
        totals = totals + lax.dot_general(term, members, contract, preferred_element_type=f32)
    counts = lax.dot_general(
        jnp.ones((16, CELLS_DEV), bf16), members, contract, preferred_element_type=f32
    )[0:1]
    result = added(
        [restrict_matrix[0:CDOF, d : d + 1] * totals[d : d + 1, :] for d in range(DOF)]
    )
    result = result / counts
    return jnp.concatenate([result[i : i + 1, :] for i in range(CDOF)], axis=1)


def first_phase_kernel(
    where_ref, first, centre, second, stencil_ref, matrix_ref,
    out, places, coefs, start_out, members_out, field, middle,
):
    odd = where_ref[2] % 2 == 1
    packs = (first, centre, second)
    fill_tables(odd, packs, places, coefs)
    fill_field(odd, packs, field)
    start = field[:, lanes_of(1 + BLOCKS, BLOCKS)]
    index_row = centre[MESH_END : MESH_END + 1, :].astype(jnp.int32)
    members = (
        lax.broadcasted_iota(jnp.int32, (COARSE_DEV, CELLS_DEV), 0) == index_row
    ).astype(f32).astype(bf16)
    members_out[...] = members
    start_out[...] = restricted(start, members, matrix_ref[...])
    march(field, middle, places, coefs, stencil_ref)
    out[...] = field[:, lanes_of(1 + BLOCKS, BLOCKS)]


def second_phase_kernel(
    where_ref, first, centre, second, places, coefs, stencil_ref, members_ref, matrix_ref, start_ref,
    out, message, field, middle,
):
    fill_field(where_ref[2] % 2 == 1, (first, centre, second), field)
    march(field, middle, places, coefs, stencil_ref)
    fine = field[:, lanes_of(1 + BLOCKS, BLOCKS)]
    out[...] = fine
    rows = jnp.concatenate(
        [restricted(fine, members_ref[...], matrix_ref[...]), start_ref[...]], axis=0
    )
    for copy in range(GROUP * PARTS):
        message[copy] = rows


def flipped(tiles, even_row):
    up = pltpu.roll(jnp.concatenate([tiles[1:], tiles[:1]], axis=0), 7, axis=1)
    down = pltpu.roll(jnp.concatenate([tiles[7:], tiles[:7]], axis=0), 1, axis=1)
    return jnp.where(even_row, up, down)


def composed(reach, inverse_ref, first, last):
    shape = (8, 8, LANES)
    row = lax.broadcasted_iota(jnp.int32, shape, 1)
    lane = lax.broadcasted_iota(jnp.int32, shape, 2)
    even_row = row % 2 == 0
    first_lane = lane == 0
    last_lane = lane == LANES - 1
    own = 1.0 - 2.0 * coupling - opposite
    blocks = []
    for by in range(CDOF):
        pieces = []
        for i in range(CDOF):
            j = (i - by) % CDOF
            for h in range(2):
                pieces.append(inverse_ref[i, j : j + 1, lanes_of(h)])
        blocks.append(jnp.concatenate(pieces, axis=0)[None])
    for repeat in range(first, last):
        swapped = {o: flipped(tiles, even_row) for o, tiles in reach.items()}
        blended = {}
        for o in range(-repeat - 1, repeat + 2):
            total = jnp.zeros(shape, f32)
            if o in reach:
                total = own * reach[o] + opposite * swapped[o]
            if o - 1 in reach:
                edge = jnp.where(last_lane, swapped[o - 1], reach[o - 1])
                total = total + coupling * pltpu.roll(edge, 1, axis=2)
            if o + 1 in reach:
                edge = jnp.where(first_lane, swapped[o + 1], reach[o + 1])
                total = total + coupling * pltpu.roll(edge, LANES - 1, axis=2)
            blended[o] = total
        reach = {}
        for o, tiles in blended.items():
            total = blocks[0] * tiles
            for by in range(1, CDOF):
                turned = jnp.concatenate([tiles[8 - 2 * by :], tiles[: 8 - 2 * by]], axis=0)
                total = total + blocks[by] * pltpu.roll(turned, 2 * by, axis=1)
            reach[o] = total
    return reach


def keep_operator(out, reach):
    size = max(reach)
    for o, tiles in reach.items():
        out[o + size] = tiles if o == 0 else pltpu.roll(tiles, -o % LANES, axis=2)


def compose_kernel(inverse_ref, out, half_way):
    turn = lax.broadcasted_iota(jnp.int32, (8, 8, LANES), 0)
    reach = composed({0: jnp.where(turn == 0, 1.0, 0.0)}, inverse_ref, 0, COARSE_STEPS)
    keep_operator(out, reach)
    reach = composed(reach, inverse_ref, COARSE_STEPS, 2 * COARSE_STEPS)
    for o, tiles in reach.items():
        half_way[o + 2 * COARSE_STEPS] = tiles


def extend_kernel(half_way, inverse_ref, out):
    size = 2 * COARSE_STEPS
    reach = {o: half_way[o + size] for o in range(-size, size + 1)}
    keep_operator(out, composed(reach, inverse_ref, size, 2 * size))


def coarse_slices(vector, operator_ref):
    turns = [vector] + [pltpu.roll(vector, d, axis=0) for d in range(1, 8)]
    reach = operator_ref.shape[0] // 2
    shares = []
    for o in range(-reach, reach + 1):
        share = added([operator_ref[o + reach, d] * turns[d] for d in range(8)])
        shares.append(share if o == 0 else pltpu.roll(share, o % LANES, axis=1))
    return added(shares)


def group_kernel(where_ref, gathered, operator_ref, ends_out, own_out, finish, start):
    group = where_ref[0]
    place = where_ref[1]
    quarter = lax.broadcasted_iota(jnp.int32, (GROUP, LANES), 1) // COARSE_DEV
    for kind, ref in enumerate((finish, start)):
        for i in range(CDOF):
            for h in range(2):
                held = jnp.zeros((GROUP, LANES), f32)
                for q in range(4):
                    p = 4 * h + q
                    rows = gathered[pl.ds(2 * p + kind, GROUP, stride=2 * PARTS), :]
                    by = (q - i) * COARSE_DEV % LANES
                    moved = rows if by == 0 else pltpu.roll(rows, by, axis=1)
                    held = jnp.where(quarter == q, moved, held)
                ref[pl.ds((2 * i + h) * GROUP, GROUP), :] = held

    def of_slice(ref, n):
        return ref[pl.ds(n, 8, stride=GROUP), :]

    chain = None
    own = jnp.zeros((8, LANES), f32)
    for n in range(GROUP):
        coarse = coarse_slices(of_slice(start, n), operator_ref)
        if n == 0:
            coarse = jnp.where(group > 0, coarse, 0.0)
        jump = of_slice(finish, n) - coarse
        chain = jump if n == 0 else coarse_slices(chain, operator_ref) + jump
        own = jnp.where(place == n, chain, own)
    for copy in range(GROUPS):
        ends_out[copy] = chain
    own_out[0] = own
    own_out[1] = finish[pl.ds(place, 8, stride=GROUP), :]


def correct_kernel(
    where_ref, ends, own_ref, operator_ref, fourfold_ref, fine_ref, members_ref, matrix_ref, out
):
    group = where_ref[0]
    place = where_ref[1]
    part = where_ref[2]

    def advance(count, vector, ref):
        return lax.fori_loop(0, count, lambda n, now: coarse_slices(now, ref), vector)

    def link(k, vector):
        return advance(GROUP // 4, vector, fourfold_ref) + ends[k]

    before = lax.fori_loop(1, group, link, ends[0])
    count = jnp.where(group > 0, place + 1, 0)
    before = advance(count % 4, advance(count // 4, before, fourfold_ref), operator_ref)
    chain = own_ref[0] + jnp.where(group > 0, before, 0.0)
    change = chain - own_ref[1]
    upper = part >= PARTS // 2
    spread = jnp.zeros((ROWS, LANES), f32)
    for i in range(CDOF):
        chosen = jnp.where(upper, change[2 * i + 1 : 2 * i + 2], change[2 * i : 2 * i + 1])
        spread = spread + matrix_ref[:, i : i + 1] * jnp.broadcast_to(chosen, (ROWS, LANES))
    spread = pltpu.roll(spread, (4 - part % 4) * COARSE_DEV % LANES, axis=1)[:, 0:COARSE_DEV]
    total = fine_ref[...]
    for term in two_terms(spread):
        total = total + jnp.dot(term, members_ref[...], preferred_element_type=f32)
    for d in range(DOF):
        out[d] = total[d : d + 1, :]


TABLE = (WINDOW + 2) * LANES
march_scratch = [pltpu.VMEM((ROWS, TABLE), f32)] * 2


params = pltpu.CompilerParams(vmem_limit_bytes=32 * 1024 * 1024)


def both_sides(values):
    pairs = [(i, i ^ 1) for i in range(PARTS)]
    others = [(i, (((i + 1) ^ 1) - 1) % PARTS) for i in range(PARTS)]
    return lax.ppermute(values, "space", pairs), lax.ppermute(values, "space", others)


smem = pl.BlockSpec(memory_space=pltpu.SMEM)


def local(
    states,
    neighbour,
    edge_x,
    edge_y,
    edge_damp,
    coriolis,
    flux_x,
    flux_y,
    rotation,
    restrict_matrix,
    prolong_matrix,
    restrict_index,
    coarse_inverse,
):
    parts = (
        states.transpose(1, 0, 2),
        neighbour,
        edge_x,
        edge_y,
        edge_damp,
        coriolis[None, :],
        restrict_index[None, :],
    )
    pack = pl.pallas_call(
        pack_kernel,
        out_shape=jax.ShapeDtypeStruct((MESH_END + 1, CELLS_DEV), f32),
        in_specs=[pl.BlockSpec(memory_space=pltpu.HBM)] * len(parts),
        out_specs=vmem,
        scratch_shapes=[pltpu.VMEM(part.shape, part.dtype) for part in parts]
        + [pltpu.SemaphoreType.DMA((len(parts),))],
        compiler_params=params,
    )(*[pltpu.with_memory_space_constraint(part, pltpu.HBM) for part in parts])
    first, second = both_sides(pack)
    slice_here = lax.axis_index("tm")
    where = jnp.stack([slice_here // GROUP, slice_here % GROUP, lax.axis_index("space")])
    where = where.astype(jnp.int32)
    wide = [jnp.pad(m, ((0, ROWS - DOF), (0, ROWS - DOF))) for m in (flux_x, flux_y, rotation)]
    stencil = jnp.concatenate(wide + [jnp.zeros((ROWS, 8), f32)], axis=1)
    high = stencil.astype(bf16)
    low = (stencil - lax.reduce_precision(stencil, 8, 7)).astype(bf16)
    stencil_terms = jnp.concatenate([high, high, low], axis=1)
    means_matrix = jnp.pad(restrict_matrix, ((0, 4), (0, LANES - DOF)))
    half, places, coefs, start, members = pl.pallas_call(
        first_phase_kernel,
        out_shape=(
            jax.ShapeDtypeStruct((ROWS, CELLS_DEV), f32),
            jax.ShapeDtypeStruct((3, 8, TABLE), jnp.int32),
            jax.ShapeDtypeStruct((10, 8, TABLE), f32),
            jax.ShapeDtypeStruct((1, LANES), f32),
            jax.ShapeDtypeStruct((COARSE_DEV, CELLS_DEV), bf16),
        ),
        in_specs=[smem] + [vmem] * 5,
        out_specs=(vmem,) * 5,
        scratch_shapes=march_scratch,
        compiler_params=params,
    )(where, first, pack, second, stencil_terms, means_matrix)
    half_first, half_second = both_sides(half)
    late_inverse, half = lax.optimization_barrier((coarse_inverse, half))
    operator, half_way = pl.pallas_call(
        compose_kernel,
        out_shape=tuple(
            jax.ShapeDtypeStruct((2 * reach + 1, 8, 8, LANES), f32)
            for reach in (COARSE_STEPS, 2 * COARSE_STEPS)
        ),
        in_specs=[vmem],
        out_specs=(vmem, vmem),
        compiler_params=params,
        cost_estimate=pl.CostEstimate(flops=12000000, bytes_accessed=900000, transcendentals=0),
    )(late_inverse)
    fine, message = pl.pallas_call(
        second_phase_kernel,
        out_shape=(
            jax.ShapeDtypeStruct((ROWS, CELLS_DEV), f32),
            pltpu.VMEM((GROUP * PARTS, 2, LANES), f32),
        ),
        in_specs=[smem] + [vmem] * 9,
        out_specs=(vmem, vmem),
        scratch_shapes=march_scratch,
        compiler_params=params,
    )(
        where, half_first, half, half_second, places, coefs, stencil_terms, members,
        means_matrix, start,
    )

    half_way, late_prolong, message = lax.optimization_barrier(
        (half_way, prolong_matrix, message)
    )
    fourfold = pl.pallas_call(
        extend_kernel,
        out_shape=jax.ShapeDtypeStruct((8 * COARSE_STEPS + 1, 8, 8, LANES), f32),
        in_specs=[vmem, vmem],
        out_specs=vmem,
        compiler_params=params,
        cost_estimate=pl.CostEstimate(flops=30000000, bytes_accessed=1700000, transcendentals=0),
    )(half_way, coarse_inverse)
    spread_matrix = jnp.pad(late_prolong, ((0, ROWS - DOF), (0, 0)))
    axes = ("tm", "space")
    count = GROUP * PARTS
    inside = [[g * count + m for m in range(count)] for g in range(GROUPS)]
    across = [[g * count + m for g in range(GROUPS)] for m in range(count)]
    gathered = lax.all_to_all(message, axes, 0, 0, tiled=True, axis_index_groups=inside)
    gathered, fourfold, spread_matrix = lax.optimization_barrier((gathered, fourfold, spread_matrix))
    ends, own = pl.pallas_call(
        group_kernel,
        out_shape=(
            jax.ShapeDtypeStruct((GROUPS, 8, LANES), f32),
            jax.ShapeDtypeStruct((2, 8, LANES), f32),
        ),
        in_specs=[smem, vmem, vmem],
        out_specs=(vmem, vmem),
        scratch_shapes=[pltpu.VMEM((8 * GROUP, LANES), f32)] * 2,
        compiler_params=params,
    )(where, gathered.reshape(GROUP * PARTS * 2, LANES), operator)
    ends = lax.all_to_all(ends, axes, 0, 0, tiled=True, axis_index_groups=across)
    updated = pl.pallas_call(
        correct_kernel,
        out_shape=jax.ShapeDtypeStruct((DOF, 1, CELLS_DEV), f32),
        in_specs=[smem] + [vmem] * 7,
        out_specs=vmem,
        compiler_params=params,
    )(where, ends, own, operator, fourfold, fine, members, spread_matrix)
    return updated.transpose(1, 0, 2)


def solution(mesh):
    in_specs = (
        P("tm", None, "space"),
        P(None, "space"),
        P(None, "space"),
        P(None, "space"),
        P(None, "space"),
        P("space"),
        P(),
        P(),
        P(),
        P(),
        P(),
        P("space"),
        P(),
    )
    out_specs = P("tm", None, "space")
    return jax.shard_map(local, mesh=mesh, in_specs=in_specs, out_specs=out_specs, check_vma=False)
```

```python
import functools

import jax
import jax.numpy as jnp
from jax import lax
from jax.experimental import pallas as pl
from jax.experimental.pallas import tpu as pltpu
from jax.sharding import PartitionSpec as P

DOF = 21
CDOF = 4
ROWS = 24
LANES = 128
HALF = 64
CELLS_DEV = 1024
COARSE_DEV = 32
COARSE_STEPS = 4
PARTS = 8
SLICES = 64
GROUP = 8
GROUPS = SLICES // GROUP
BLOCKS = CELLS_DEV // LANES
PHASE_STEPS = 8
WINDOW = 3 * BLOCKS
MESH_END = DOF + 13

coupling = 0.1
opposite = 0.25
highest = lax.Precision.HIGHEST
f32 = jnp.float32
bf16 = jnp.bfloat16
vmem = pl.BlockSpec(memory_space=pltpu.VMEM)


def lane_gather(values, index):
    numbers = lax.GatherDimensionNumbers(
        offset_dims=(),
        collapsed_slice_dims=(1,),
        start_index_map=(1,),
        operand_batching_dims=(0,),
        start_indices_batching_dims=(0,),
    )
    return lax.gather(
        values, index[..., None], numbers, (1, 1), mode=lax.GatherScatterMode.PROMISE_IN_BOUNDS
    )


def two_terms(values):
    high = values.astype(bf16)
    return high, (values - high.astype(f32)).astype(bf16)


def lanes_of(block, count=1):
    return slice(block * LANES, (block + count) * LANES)


def sides(odd, first, second, rows):
    one, two = first[rows, :], second[rows, :]
    return jnp.where(odd, one, two), jnp.where(odd, two, one)


def in_order(odd, refs, rows):
    left, right = sides(odd, refs[0], refs[2], rows)
    return left, refs[1][rows, :], right


def fill_field(odd, state_refs, field):
    inside = lax.broadcasted_iota(jnp.int32, (ROWS, CELLS_DEV), 0) < DOF
    edge = jnp.zeros((ROWS, LANES), f32)
    field[:, lanes_of(0)] = edge
    field[:, lanes_of(WINDOW + 1)] = edge
    for part, state in enumerate(in_order(odd, state_refs, slice(0, ROWS))):
        field[:, lanes_of(1 + part * BLOCKS, BLOCKS)] = jnp.where(inside, state, 0.0)


def fill_tables(odd, mesh_refs, places, coefs):
    lane = lax.broadcasted_iota(jnp.int32, (8, CELLS_DEV), 1) % LANES
    for part, mesh in enumerate(in_order(odd, mesh_refs, slice(DOF, MESH_END))):
        cells = lanes_of(1 + part * BLOCKS, BLOCKS)
        for e in range(3):
            offset = mesh[e : e + 1, :].astype(jnp.int32)
            target = jnp.broadcast_to(offset, (8, CELLS_DEV)) + lane
            within = (target >= 0) & (target < LANES)
            places[e, :, cells] = (target & (LANES - 1)) + jnp.where(within, 0, LANES)
        for row in range(10):
            coefs[row, :, cells] = jnp.broadcast_to(mesh[3 + row : 4 + row, :], (8, CELLS_DEV))


def block_rate(source, block, places, coefs, stencil, low_half):
    here = lanes_of(block)
    centre = []
    around = []
    for r in range(3):
        rows = slice(8 * r, 8 * r + 8)
        centre.append(source[rows, here])
        around.append(
            jnp.where(low_half, source[rows, lanes_of(block + 1)], source[rows, lanes_of(block - 1)])
        )
    sums = [[None] * 3 for _ in range(3)]
    for e in range(3):
        place = places[e, :, here]
        index = place & (LANES - 1)
        within = place < LANES
        found = [lane_gather(piece, index) for piece in centre + around]
        for r in range(3):
            difference = jnp.where(within, found[r], found[3 + r]) - centre[r]
            for a in range(3):
                term = coefs[3 * a + e, :, here] * difference
                sums[a][r] = term if e == 0 else sums[a][r] + term
    turned = [coefs[9, :, here] * piece for piece in centre]
    stacked = jnp.concatenate(sums[0] + sums[1] + turned + [jnp.zeros((8, LANES), f32)], axis=0)
    high, low = two_terms(stacked)
    mixed = jnp.dot(
        stencil, jnp.concatenate([high, low, high], axis=0), preferred_element_type=f32
    )
    return mixed + jnp.concatenate(sums[2], axis=0)


def march(field, middle, places, coefs, stencil_ref):
    low_half = lax.broadcasted_iota(jnp.int32, (8, LANES), 1) < HALF
    edge = jnp.zeros((ROWS, LANES), f32)
    middle[:, lanes_of(0)] = edge
    middle[:, lanes_of(WINDOW + 1)] = edge

    stencil = stencil_ref[...]
    for index in range(PHASE_STEPS):
        for b in range(1 + index, 1 + WINDOW - index):
            rate = block_rate(field, b, places, coefs, stencil, low_half)
            middle[:, lanes_of(b)] = field[:, lanes_of(b)] + rate
        for b in range(2 + index, WINDOW - index):
            rate = block_rate(middle, b, places, coefs, stencil, low_half)
            here = lanes_of(b)
            field[:, here] = 0.5 * (field[:, here] + middle[:, here] + rate)


def pack_kernel(*refs):
    sources, out, buffers, done = refs[:7], refs[7], refs[8:15], refs[15]
    copies = [
        pltpu.make_async_copy(source, buffer, done.at[i])
        for i, (source, buffer) in enumerate(zip(sources, buffers))
    ]
    for copy in copies:
        copy.start()
    row = 0
    for copy, buffer in zip(copies, buffers):
        copy.wait()
        if len(buffer.shape) == 3:
            for d in range(DOF):
                out[d : d + 1, :] = buffer[d]
            row = DOF
        else:
            count = buffer.shape[0]
            out[row : row + count, :] = buffer[...].astype(f32)
            row += count


def added(terms):
    while len(terms) > 1:
        terms = [sum(terms[i : i + 2][1:], terms[i]) for i in range(0, len(terms), 2)]
    return terms[0]


def restricted(values, members, restrict_matrix):
    contract = (((1,), (1,)), ((), ()))
    totals = jnp.zeros((ROWS, COARSE_DEV), f32)
    for term in two_terms(values):
        totals = totals + lax.dot_general(term, members, contract, preferred_element_type=f32)
    counts = lax.dot_general(
        jnp.ones((16, CELLS_DEV), bf16), members, contract, preferred_element_type=f32
    )[0:1]
    result = added(
        [restrict_matrix[0:CDOF, d : d + 1] * totals[d : d + 1, :] for d in range(DOF)]
    )
    result = result / counts
    return jnp.concatenate([result[i : i + 1, :] for i in range(CDOF)], axis=1)


def prepare_kernel(*refs):
    sources, outs, buffers, done = refs[:6], refs[6:10], refs[10:15], refs[15]
    stencil_out, means_out, spread_out, inverse_out = outs
    copies = [
        pltpu.make_async_copy(source, buffer, done.at[i])
        for i, (source, buffer) in enumerate(zip(sources, buffers + (inverse_out,)))
    ]
    for copy in copies:
        copy.start()
    for copy in copies:
        copy.wait()
    flux_x, flux_y, rotation, means, spread = [buffer[...] for buffer in buffers]
    side = ROWS - DOF
    wide = [jnp.pad(m, ((0, side), (0, side))) for m in (flux_x, flux_y, rotation)]
    stencil = jnp.concatenate(wide + [jnp.zeros((ROWS, 8), f32)], axis=1)
    high = stencil.astype(bf16).astype(f32)
    stencil_out[...] = jnp.concatenate([high, high, stencil - high], axis=1).astype(bf16)
    means_out[...] = jnp.pad(means, ((0, 8 - CDOF), (0, LANES - DOF)))
    turned = jnp.pad(spread, ((0, 8 - CDOF), (0, LANES - DOF))).T
    spread_out[...] = turned[0:ROWS, :]


def first_phase_kernel(
    where_ref, first, centre, second, stencil_ref, matrix_ref,
    out, places, coefs, start_out, members_out, field, middle,
):
    odd = where_ref[2] % 2 == 1
    packs = (first, centre, second)
    fill_tables(odd, packs, places, coefs)
    fill_field(odd, packs, field)
    start = field[:, lanes_of(1 + BLOCKS, BLOCKS)]
    index_row = centre[MESH_END : MESH_END + 1, :].astype(jnp.int32)
    members = (
        lax.broadcasted_iota(jnp.int32, (COARSE_DEV, CELLS_DEV), 0) == index_row
    ).astype(f32).astype(bf16)
    members_out[...] = members
    start_out[...] = restricted(start, members, matrix_ref[...])
    march(field, middle, places, coefs, stencil_ref)
    out[...] = field[:, lanes_of(1 + BLOCKS, BLOCKS)]


def second_phase_kernel(
    where_ref, first, centre, second, places, coefs, stencil_ref, members_ref, matrix_ref, start_ref,
    out, message, field, middle,
):
    fill_field(where_ref[2] % 2 == 1, (first, centre, second), field)
    march(field, middle, places, coefs, stencil_ref)
    fine = field[:, lanes_of(1 + BLOCKS, BLOCKS)]
    out[...] = fine
    rows = jnp.concatenate(
        [restricted(fine, members_ref[...], matrix_ref[...]), start_ref[...]], axis=0
    )
    for copy in range(GROUP * PARTS):
        message[copy] = rows


def flipped(tiles, even_row):
    up = pltpu.roll(jnp.concatenate([tiles[1:], tiles[:1]], axis=0), 7, axis=1)
    down = pltpu.roll(jnp.concatenate([tiles[7:], tiles[:7]], axis=0), 1, axis=1)
    return jnp.where(even_row, up, down)


def compose_kernel(inverse_ref, out, out_twice):
    shape = (8, 8, LANES)
    row = lax.broadcasted_iota(jnp.int32, shape, 1)
    lane = lax.broadcasted_iota(jnp.int32, shape, 2)
    turn = lax.broadcasted_iota(jnp.int32, shape, 0)
    even_row = row % 2 == 0
    first_lane = lane == 0
    last_lane = lane == LANES - 1
    own = 1.0 - 2.0 * coupling - opposite
    blocks = []
    for by in range(CDOF):
        pieces = []
        for i in range(CDOF):
            j = (i - by) % CDOF
            for h in range(2):
                pieces.append(inverse_ref[i, j : j + 1, lanes_of(h)])
        blocks.append(jnp.concatenate(pieces, axis=0)[None])
    reach = {0: jnp.where(turn == 0, 1.0, 0.0)}
    for repeat in range(2 * COARSE_STEPS):
        swapped = {o: flipped(tiles, even_row) for o, tiles in reach.items()}
        blended = {}
        for o in range(-repeat - 1, repeat + 2):
            total = jnp.zeros(shape, f32)
            if o in reach:
                total = own * reach[o] + opposite * swapped[o]
            if o - 1 in reach:
                edge = jnp.where(last_lane, swapped[o - 1], reach[o - 1])
                total = total + coupling * pltpu.roll(edge, 1, axis=2)
            if o + 1 in reach:
                edge = jnp.where(first_lane, swapped[o + 1], reach[o + 1])
                total = total + coupling * pltpu.roll(edge, LANES - 1, axis=2)
            blended[o] = total
        reach = {}
        for o, tiles in blended.items():
            total = blocks[0] * tiles
            for by in range(1, CDOF):
                turned = jnp.concatenate([tiles[8 - 2 * by :], tiles[: 8 - 2 * by]], axis=0)
                total = total + blocks[by] * pltpu.roll(turned, 2 * by, axis=1)
            reach[o] = total
        if (repeat + 1) % COARSE_STEPS == 0:
            held = out if repeat < COARSE_STEPS else out_twice
            for o, tiles in reach.items():
                held[o + repeat + 1] = tiles if o == 0 else pltpu.roll(tiles, -o % LANES, axis=2)


def coarse_slice(vector, operator_ref):
    turns = [vector] + [pltpu.roll(vector, d, axis=0) for d in range(1, 8)]
    reach = operator_ref.shape[0] // 2
    shares = []
    for o in range(-reach, reach + 1):
        share = added([operator_ref[o + reach, d] * turns[d] for d in range(8)])
        shares.append(share if o == 0 else pltpu.roll(share, o % LANES, axis=1))
    return added(shares)


def group_kernel(where_ref, gathered, operator_ref, ends_out, own_out, finish, start):
    group = where_ref[0]
    place = where_ref[1]
    quarter = lax.broadcasted_iota(jnp.int32, (GROUP, LANES), 1) // COARSE_DEV
    for kind, ref in enumerate((finish, start)):
        for i in range(CDOF):
            for h in range(2):
                held = jnp.zeros((GROUP, LANES), f32)
                for q in range(4):
                    p = 4 * h + q
                    rows = gathered[pl.ds(2 * p + kind, GROUP, stride=2 * PARTS), :]
                    by = (q - i) * COARSE_DEV % LANES
                    moved = rows if by == 0 else pltpu.roll(rows, by, axis=1)
                    held = jnp.where(quarter == q, moved, held)
                ref[pl.ds((2 * i + h) * GROUP, GROUP), :] = held

    def of_slice(ref, n):
        return ref[pl.ds(n, 8, stride=GROUP), :]

    chain = None
    own = jnp.zeros((8, LANES), f32)
    for n in range(GROUP):
        coarse = coarse_slice(of_slice(start, n), operator_ref)
        if n == 0:
            coarse = jnp.where(group > 0, coarse, 0.0)
        jump = of_slice(finish, n) - coarse
        chain = jump if n == 0 else coarse_slice(chain, operator_ref) + jump
        own = jnp.where(place == n, chain, own)
    for copy in range(GROUPS):
        ends_out[copy] = chain
    own_out[0] = own
    own_out[1] = finish[pl.ds(place, 8, stride=GROUP), :]


def correct_kernel(
    where_ref, ends, own_ref, operator_ref, twice_ref, fine_ref, members_ref, matrix_ref, out
):
    group = where_ref[0]
    place = where_ref[1]
    part = where_ref[2]

    def advance(count, vector, ref):
        return lax.fori_loop(0, count, lambda n, now: coarse_slice(now, ref), vector)

    def link(k, vector):
        return advance(GROUP // 2, vector, twice_ref) + ends[k]

    before = lax.fori_loop(1, group, link, ends[0])
    count = jnp.where(group > 0, place + 1, 0)
    before = advance(count % 2, advance(count // 2, before, twice_ref), operator_ref)
    chain = own_ref[0] + jnp.where(group > 0, before, 0.0)
    change = chain - own_ref[1]
    upper = part >= PARTS // 2
    spread = jnp.zeros((ROWS, LANES), f32)
    for i in range(CDOF):
        chosen = jnp.where(upper, change[2 * i + 1 : 2 * i + 2], change[2 * i : 2 * i + 1])
        spread = spread + matrix_ref[:, i : i + 1] * jnp.broadcast_to(chosen, (ROWS, LANES))
    spread = pltpu.roll(spread, (4 - part % 4) * COARSE_DEV % LANES, axis=1)[:, 0:COARSE_DEV]
    total = fine_ref[...]
    for term in two_terms(spread):
        total = total + jnp.dot(term, members_ref[...], preferred_element_type=f32)
    for d in range(DOF):
        out[d] = total[d : d + 1, :]


TABLE = (WINDOW + 2) * LANES
march_scratch = [pltpu.VMEM((ROWS, TABLE), f32)] * 2


params = pltpu.CompilerParams(vmem_limit_bytes=32 * 1024 * 1024)


def both_sides(values):
    pairs = [(i, i ^ 1) for i in range(PARTS)]
    others = [(i, (((i + 1) ^ 1) - 1) % PARTS) for i in range(PARTS)]
    return lax.ppermute(values, "space", pairs), lax.ppermute(values, "space", others)


smem = pl.BlockSpec(memory_space=pltpu.SMEM)


def local(
    states,
    neighbour,
    edge_x,
    edge_y,
    edge_damp,
    coriolis,
    flux_x,
    flux_y,
    rotation,
    restrict_matrix,
    prolong_matrix,
    restrict_index,
    coarse_inverse,
):
    parts = (
        states.transpose(1, 0, 2),
        neighbour,
        edge_x,
        edge_y,
        edge_damp,
        coriolis[None, :],
        restrict_index[None, :],
    )
    pack = pl.pallas_call(
        pack_kernel,
        out_shape=jax.ShapeDtypeStruct((MESH_END + 1, CELLS_DEV), f32),
        in_specs=[pl.BlockSpec(memory_space=pltpu.HBM)] * len(parts),
        out_specs=vmem,
        scratch_shapes=[pltpu.VMEM(part.shape, part.dtype) for part in parts]
        + [pltpu.SemaphoreType.DMA((len(parts),))],
        compiler_params=params,
    )(*[pltpu.with_memory_space_constraint(part, pltpu.HBM) for part in parts])
    first, second = both_sides(pack)
    slice_here = lax.axis_index("tm")
    where = jnp.stack([slice_here // GROUP, slice_here % GROUP, lax.axis_index("space")])
    where = where.astype(jnp.int32)
    small = (flux_x, flux_y, rotation, restrict_matrix, prolong_matrix.T, coarse_inverse)
    stencil_terms, means_matrix, spread_matrix, near_inverse = pl.pallas_call(
        prepare_kernel,
        out_shape=(
            jax.ShapeDtypeStruct((ROWS, 240), bf16),
            jax.ShapeDtypeStruct((8, LANES), f32),
            jax.ShapeDtypeStruct((ROWS, 8), f32),
            jax.ShapeDtypeStruct(coarse_inverse.shape, f32),
        ),
        in_specs=[pl.BlockSpec(memory_space=pltpu.HBM)] * len(small),
        out_specs=(vmem,) * 4,
        scratch_shapes=[pltpu.VMEM(part.shape, part.dtype) for part in small[:5]]
        + [pltpu.SemaphoreType.DMA((len(small),))],
        compiler_params=params,
        cost_estimate=pl.CostEstimate(flops=2000000, bytes_accessed=200000, transcendentals=0),
    )(*[pltpu.with_memory_space_constraint(part, pltpu.HBM) for part in small])
    half, places, coefs, start, members = pl.pallas_call(
        first_phase_kernel,
        out_shape=(
            jax.ShapeDtypeStruct((ROWS, CELLS_DEV), f32),
            jax.ShapeDtypeStruct((3, 8, TABLE), jnp.int32),
            jax.ShapeDtypeStruct((10, 8, TABLE), f32),
            jax.ShapeDtypeStruct((1, LANES), f32),
            jax.ShapeDtypeStruct((COARSE_DEV, CELLS_DEV), bf16),
        ),
        in_specs=[smem] + [vmem] * 5,
        out_specs=(vmem,) * 5,
        scratch_shapes=march_scratch,
        compiler_params=params,
    )(where, first, pack, second, stencil_terms, means_matrix)
    half_first, half_second = both_sides(half)
    late_inverse, half = lax.optimization_barrier((near_inverse, half))
    operator, operator_twice = pl.pallas_call(
        compose_kernel,
        out_shape=tuple(
            jax.ShapeDtypeStruct((2 * reach + 1, 8, 8, LANES), f32)
            for reach in (COARSE_STEPS, 2 * COARSE_STEPS)
        ),
        in_specs=[vmem],
        out_specs=(vmem, vmem),
        compiler_params=params,
        cost_estimate=pl.CostEstimate(flops=12000000, bytes_accessed=900000, transcendentals=0),
    )(late_inverse)
    fine, message = pl.pallas_call(
        second_phase_kernel,
        out_shape=(
            jax.ShapeDtypeStruct((ROWS, CELLS_DEV), f32),
            jax.ShapeDtypeStruct((GROUP * PARTS, 2, LANES), f32),
        ),
        in_specs=[smem] + [vmem] * 9,
        out_specs=(vmem, vmem),
        scratch_shapes=march_scratch,
        compiler_params=params,
    )(
        where, half_first, half, half_second, places, coefs, stencil_terms, members,
        means_matrix, start,
    )

    message, operator, operator_twice, spread_matrix = lax.optimization_barrier(
        (message, operator, operator_twice, spread_matrix)
    )
    axes = ("tm", "space")
    count = GROUP * PARTS
    inside = [[g * count + m for m in range(count)] for g in range(GROUPS)]
    across = [[g * count + m for g in range(GROUPS)] for m in range(count)]
    gathered = lax.all_to_all(message, axes, 0, 0, tiled=True, axis_index_groups=inside)
    ends, own = pl.pallas_call(
        group_kernel,
        out_shape=(
            jax.ShapeDtypeStruct((GROUPS, 8, LANES), f32),
            jax.ShapeDtypeStruct((2, 8, LANES), f32),
        ),
        in_specs=[smem, vmem, vmem],
        out_specs=(vmem, vmem),
        scratch_shapes=[pltpu.VMEM((8 * GROUP, LANES), f32)] * 2,
        compiler_params=params,
    )(where, gathered.reshape(GROUP * PARTS * 2, LANES), operator)
    ends = lax.all_to_all(ends, axes, 0, 0, tiled=True, axis_index_groups=across)
    updated = pl.pallas_call(
        correct_kernel,
        out_shape=jax.ShapeDtypeStruct((DOF, 1, CELLS_DEV), f32),
        in_specs=[smem] + [vmem] * 7,
        out_specs=vmem,
        compiler_params=params,
    )(where, ends, own, operator, operator_twice, fine, members, spread_matrix)
    return updated.transpose(1, 0, 2)


def solution(mesh):
    in_specs = (
        P("tm", None, "space"),
        P(None, "space"),
        P(None, "space"),
        P(None, "space"),
        P(None, "space"),
        P("space"),
        P(),
        P(),
        P(),
        P(),
        P(),
        P("space"),
        P(),
    )
    out_specs = P("tm", None, "space")
    return jax.shard_map(local, mesh=mesh, in_specs=in_specs, out_specs=out_specs, check_vma=False)
```

```python
import functools

import jax
import jax.numpy as jnp
from jax import lax
from jax.experimental import pallas as pl
from jax.experimental.pallas import tpu as pltpu
from jax.sharding import PartitionSpec as P

DOF = 21
CDOF = 4
ROWS = 24
LANES = 128
HALF = 64
CELLS_DEV = 1024
COARSE_DEV = 32
COARSE_STEPS = 4
PARTS = 8
SLICES = 64
GROUP = 8
GROUPS = SLICES // GROUP
BLOCKS = CELLS_DEV // LANES
PHASE_STEPS = 8
WINDOW = 3 * BLOCKS
MESH_END = DOF + 13

coupling = 0.1
opposite = 0.25
highest = lax.Precision.HIGHEST
f32 = jnp.float32
bf16 = jnp.bfloat16
vmem = pl.BlockSpec(memory_space=pltpu.VMEM)


def lane_gather(values, index):
    numbers = lax.GatherDimensionNumbers(
        offset_dims=(),
        collapsed_slice_dims=(1,),
        start_index_map=(1,),
        operand_batching_dims=(0,),
        start_indices_batching_dims=(0,),
    )
    return lax.gather(
        values, index[..., None], numbers, (1, 1), mode=lax.GatherScatterMode.PROMISE_IN_BOUNDS
    )


def two_terms(values):
    high = values.astype(bf16)
    return high, (values - high.astype(f32)).astype(bf16)


def lanes_of(block, count=1):
    return slice(block * LANES, (block + count) * LANES)


def in_order(odd, refs, place):
    one, two = refs[0][place], refs[2][place]
    return jnp.where(odd, one, two), refs[1][place], jnp.where(odd, two, one)


def fill_field(odd, state_refs, field):
    edge = jnp.zeros((ROWS, LANES), f32)
    field[:, lanes_of(0)] = edge
    field[:, lanes_of(WINDOW + 1)] = edge
    rest = jnp.zeros((ROWS - DOF, LANES), f32)
    for b in range(BLOCKS):
        whole = in_order(odd, state_refs, (slice(0, 16), b, slice(None)))
        tail = in_order(odd, state_refs, (slice(16, DOF), b, slice(None)))
        for part in range(3):
            here = lanes_of(1 + part * BLOCKS + b)
            field[0:16, here] = whole[part]
            field[16:ROWS, here] = jnp.concatenate([tail[part], rest], axis=0)


def fill_tables(odd, mesh_refs, places, coefs):
    lane = lax.broadcasted_iota(jnp.int32, (BLOCKS, LANES), 1)

    def spread(table, row, part, tile):
        for b in range(BLOCKS):
            here = lanes_of(1 + part * BLOCKS + b)
            table[row, :, here] = jnp.broadcast_to(tile[b : b + 1, :], (8, LANES))

    for row in range(MESH_END - DOF):
        for part, tile in enumerate(in_order(odd, mesh_refs, DOF + row)):
            if row < 3:
                target = tile.astype(jnp.int32) + lane
                within = (target >= 0) & (target < LANES)
                spread(
                    places, row, part, (target & (LANES - 1)) + jnp.where(within, 0, LANES)
                )
            else:
                spread(coefs, row - 3, part, tile)


def block_rate(source, block, places, coefs, stencil, low_half):
    here = lanes_of(block)
    centre = []
    around = []
    for r in range(3):
        rows = slice(8 * r, 8 * r + 8)
        centre.append(source[rows, here])
        around.append(
            jnp.where(low_half, source[rows, lanes_of(block + 1)], source[rows, lanes_of(block - 1)])
        )
    sums = [[None] * 3 for _ in range(3)]
    for e in range(3):
        place = places[e, :, here]
        index = place & (LANES - 1)
        within = place < LANES
        found = [lane_gather(piece, index) for piece in centre + around]
        for r in range(3):
            difference = jnp.where(within, found[r], found[3 + r]) - centre[r]
            for a in range(3):
                term = coefs[3 * a + e, :, here] * difference
                sums[a][r] = term if e == 0 else sums[a][r] + term
    turned = [coefs[9, :, here] * piece for piece in centre]
    stacked = jnp.concatenate(sums[0] + sums[1] + turned + [jnp.zeros((8, LANES), f32)], axis=0)
    high, low = two_terms(stacked)
    mixed = jnp.dot(
        stencil, jnp.concatenate([high, low, high], axis=0), preferred_element_type=f32
    )
    return mixed + jnp.concatenate(sums[2], axis=0)


def march(field, middle, places, coefs, stencil_ref):
    low_half = lax.broadcasted_iota(jnp.int32, (8, LANES), 1) < HALF
    edge = jnp.zeros((ROWS, LANES), f32)
    middle[:, lanes_of(0)] = edge
    middle[:, lanes_of(WINDOW + 1)] = edge

    stencil = stencil_ref[...]
    for index in range(PHASE_STEPS):
        for b in range(1 + index, 1 + WINDOW - index):
            rate = block_rate(field, b, places, coefs, stencil, low_half)
            middle[:, lanes_of(b)] = field[:, lanes_of(b)] + rate
        for b in range(2 + index, WINDOW - index):
            rate = block_rate(middle, b, places, coefs, stencil, low_half)
            here = lanes_of(b)
            field[:, here] = 0.5 * (field[:, here] + middle[:, here] + rate)


def pack_kernel(states, coriolis, neighbour, edge_x, edge_y, edge_damp, out, *scratch):
    buffers, done = scratch[:4], scratch[4]
    last = MESH_END - 1
    pairs = [(states, out.at[0:DOF]), (coriolis, out.at[last : last + 1])]
    pairs += list(zip((neighbour, edge_x, edge_y, edge_damp), buffers))
    copies = [
        pltpu.make_async_copy(source, target, done.at[i])
        for i, (source, target) in enumerate(pairs)
    ]
    for copy in copies:
        copy.start()
    for copy in copies:
        copy.wait()
    for i, buffer in enumerate(buffers):
        rows = buffer[...].astype(f32)
        for e in range(3):
            for b in range(BLOCKS):
                out[DOF + 3 * i + e, b : b + 1, :] = rows[e : e + 1, lanes_of(b)]


def added(terms):
    while len(terms) > 1:
        terms = [sum(terms[i : i + 2][1:], terms[i]) for i in range(0, len(terms), 2)]
    return terms[0]


def restricted(values, members, restrict_matrix):
    contract = (((1,), (1,)), ((), ()))
    totals = jnp.zeros((ROWS, COARSE_DEV), f32)
    for term in two_terms(values):
        totals = totals + lax.dot_general(term, members, contract, preferred_element_type=f32)
    counts = lax.dot_general(
        jnp.ones((16, CELLS_DEV), bf16), members, contract, preferred_element_type=f32
    )[0:1]
    result = added(
        [restrict_matrix[0:CDOF, d : d + 1] * totals[d : d + 1, :] for d in range(DOF)]
    )
    result = result / counts
    return jnp.concatenate([result[i : i + 1, :] for i in range(CDOF)], axis=1)


def prepare_kernel(*refs):
    sources, outs, buffers, done = refs[:7], refs[7:12], refs[12:18], refs[18]
    stencil_out, means_out, spread_out, members_out, inverse_out = outs
    copies = [
        pltpu.make_async_copy(source, buffer, done.at[i])
        for i, (source, buffer) in enumerate(zip(sources, buffers + (inverse_out,)))
    ]
    for copy in copies:
        copy.start()
    for copy in copies:
        copy.wait()
    flux_x, flux_y, rotation, means, spread, index = [buffer[...] for buffer in buffers]
    side = ROWS - DOF
    wide = [jnp.pad(m, ((0, side), (0, side))) for m in (flux_x, flux_y, rotation)]
    stencil = jnp.concatenate(wide + [jnp.zeros((ROWS, 8), f32)], axis=1)
    high = stencil.astype(bf16).astype(f32)
    stencil_out[...] = jnp.concatenate([high, high, stencil - high], axis=1).astype(bf16)
    means_out[...] = jnp.pad(means, ((0, 8 - CDOF), (0, LANES - DOF)))
    turned = jnp.pad(spread, ((0, 8 - CDOF), (0, LANES - DOF))).T
    spread_out[...] = turned[0:ROWS, :]
    members = lax.broadcasted_iota(jnp.int32, (COARSE_DEV, CELLS_DEV), 0) == index
    members_out[...] = members.astype(f32).astype(bf16)


def first_phase_kernel(
    where_ref, first, centre, second, stencil_ref, members_ref, matrix_ref,
    out, places, coefs, start_out, field, middle,
):
    odd = where_ref[2] % 2 == 1
    packs = (first, centre, second)
    fill_tables(odd, packs, places, coefs)
    fill_field(odd, packs, field)
    start = field[:, lanes_of(1 + BLOCKS, BLOCKS)]
    start_out[...] = restricted(start, members_ref[...], matrix_ref[...])
    march(field, middle, places, coefs, stencil_ref)
    for b in range(BLOCKS):
        out[:, b, :] = field[0:DOF, lanes_of(1 + BLOCKS + b)]


def second_phase_kernel(
    where_ref, first, centre, second, places, coefs, stencil_ref, members_ref, matrix_ref, start_ref,
    out, message, field, middle,
):
    fill_field(where_ref[2] % 2 == 1, (first, centre, second), field)
    march(field, middle, places, coefs, stencil_ref)
    fine = field[:, lanes_of(1 + BLOCKS, BLOCKS)]
    out[...] = fine
    rows = jnp.concatenate(
        [restricted(fine, members_ref[...], matrix_ref[...]), start_ref[...]], axis=0
    )
    for copy in range(GROUP * PARTS):
        message[copy] = rows


def flipped(tiles, even_row):
    up = pltpu.roll(jnp.concatenate([tiles[1:], tiles[:1]], axis=0), 7, axis=1)
    down = pltpu.roll(jnp.concatenate([tiles[7:], tiles[:7]], axis=0), 1, axis=1)
    return jnp.where(even_row, up, down)


def compose_kernel(inverse_ref, out, out_twice):
    shape = (8, 8, LANES)
    row = lax.broadcasted_iota(jnp.int32, shape, 1)
    lane = lax.broadcasted_iota(jnp.int32, shape, 2)
    turn = lax.broadcasted_iota(jnp.int32, shape, 0)
    even_row = row % 2 == 0
    first_lane = lane == 0
    last_lane = lane == LANES - 1
    own = 1.0 - 2.0 * coupling - opposite
    blocks = []
    for by in range(CDOF):
        pieces = []
        for i in range(CDOF):
            j = (i - by) % CDOF
            for h in range(2):
                pieces.append(inverse_ref[i, j : j + 1, lanes_of(h)])
        blocks.append(jnp.concatenate(pieces, axis=0)[None])
    reach = {0: jnp.where(turn == 0, 1.0, 0.0)}
    for repeat in range(2 * COARSE_STEPS):
        swapped = {o: flipped(tiles, even_row) for o, tiles in reach.items()}
        blended = {}
        for o in range(-repeat - 1, repeat + 2):
            total = jnp.zeros(shape, f32)
            if o in reach:
                total = own * reach[o] + opposite * swapped[o]
            if o - 1 in reach:
                edge = jnp.where(last_lane, swapped[o - 1], reach[o - 1])
                total = total + coupling * pltpu.roll(edge, 1, axis=2)
            if o + 1 in reach:
                edge = jnp.where(first_lane, swapped[o + 1], reach[o + 1])
                total = total + coupling * pltpu.roll(edge, LANES - 1, axis=2)
            blended[o] = total
        reach = {}
        for o, tiles in blended.items():
            total = blocks[0] * tiles
            for by in range(1, CDOF):
                turned = jnp.concatenate([tiles[8 - 2 * by :], tiles[: 8 - 2 * by]], axis=0)
                total = total + blocks[by] * pltpu.roll(turned, 2 * by, axis=1)
            reach[o] = total
        if (repeat + 1) % COARSE_STEPS == 0:
            held = out if repeat < COARSE_STEPS else out_twice
            for o, tiles in reach.items():
                held[o + repeat + 1] = tiles if o == 0 else pltpu.roll(tiles, -o % LANES, axis=2)


def coarse_slice(vector, operator_ref):
    turns = [vector] + [pltpu.roll(vector, d, axis=0) for d in range(1, 8)]
    reach = operator_ref.shape[0] // 2
    shares = []
    for o in range(-reach, reach + 1):
        share = added([operator_ref[o + reach, d] * turns[d] for d in range(8)])
        shares.append(share if o == 0 else pltpu.roll(share, o % LANES, axis=1))
    return added(shares)


def group_kernel(where_ref, gathered, operator_ref, ends_out, own_out, finish, start):
    group = where_ref[0]
    place = where_ref[1]
    quarter = lax.broadcasted_iota(jnp.int32, (GROUP, LANES), 1) // COARSE_DEV
    for kind, ref in enumerate((finish, start)):
        for i in range(CDOF):
            for h in range(2):
                held = jnp.zeros((GROUP, LANES), f32)
                for q in range(4):
                    p = 4 * h + q
                    rows = gathered[pl.ds(2 * p + kind, GROUP, stride=2 * PARTS), :]
                    by = (q - i) * COARSE_DEV % LANES
                    moved = rows if by == 0 else pltpu.roll(rows, by, axis=1)
                    held = jnp.where(quarter == q, moved, held)
                ref[pl.ds((2 * i + h) * GROUP, GROUP), :] = held

    def of_slice(ref, n):
        return ref[pl.ds(n, 8, stride=GROUP), :]

    chain = None
    own = jnp.zeros((8, LANES), f32)
    for n in range(GROUP):
        coarse = coarse_slice(of_slice(start, n), operator_ref)
        if n == 0:
            coarse = jnp.where(group > 0, coarse, 0.0)
        jump = of_slice(finish, n) - coarse
        chain = jump if n == 0 else coarse_slice(chain, operator_ref) + jump
        own = jnp.where(place == n, chain, own)
    for copy in range(GROUPS):
        ends_out[copy] = chain
    own_out[0] = own
    own_out[1] = finish[pl.ds(place, 8, stride=GROUP), :]


def correct_kernel(
    where_ref, ends, own_ref, operator_ref, twice_ref, fine_ref, members_ref, matrix_ref, out
):
    group = where_ref[0]
    place = where_ref[1]
    part = where_ref[2]

    def advance(count, vector, ref):
        return lax.fori_loop(0, count, lambda n, now: coarse_slice(now, ref), vector)

    def link(k, vector):
        return advance(GROUP // 2, vector, twice_ref) + ends[k]

    before = lax.fori_loop(1, group, link, ends[0])
    count = jnp.where(group > 0, place + 1, 0)
    before = advance(count % 2, advance(count // 2, before, twice_ref), operator_ref)
    chain = own_ref[0] + jnp.where(group > 0, before, 0.0)
    change = chain - own_ref[1]
    upper = part >= PARTS // 2
    spread = jnp.zeros((ROWS, LANES), f32)
    for i in range(CDOF):
        chosen = jnp.where(upper, change[2 * i + 1 : 2 * i + 2], change[2 * i : 2 * i + 1])
        spread = spread + matrix_ref[:, i : i + 1] * jnp.broadcast_to(chosen, (ROWS, LANES))
    spread = pltpu.roll(spread, (4 - part % 4) * COARSE_DEV % LANES, axis=1)[:, 0:COARSE_DEV]
    total = fine_ref[...]
    for term in two_terms(spread):
        total = total + jnp.dot(term, members_ref[...], preferred_element_type=f32)
    for d in range(DOF):
        out[d] = total[d : d + 1, :]


TABLE = (WINDOW + 2) * LANES
march_scratch = [pltpu.VMEM((ROWS, TABLE), f32)] * 2


params = pltpu.CompilerParams(vmem_limit_bytes=32 * 1024 * 1024)


def both_sides(values):
    pairs = [(i, i ^ 1) for i in range(PARTS)]
    others = [(i, (((i + 1) ^ 1) - 1) % PARTS) for i in range(PARTS)]
    return lax.ppermute(values, "space", pairs), lax.ppermute(values, "space", others)


smem = pl.BlockSpec(memory_space=pltpu.SMEM)


def local(
    states,
    neighbour,
    edge_x,
    edge_y,
    edge_damp,
    coriolis,
    flux_x,
    flux_y,
    rotation,
    restrict_matrix,
    prolong_matrix,
    restrict_index,
    coarse_inverse,
):
    parts = (
        states.transpose(1, 0, 2).reshape(DOF, BLOCKS, LANES),
        coriolis.reshape(1, BLOCKS, LANES),
        neighbour,
        edge_x,
        edge_y,
        edge_damp,
    )
    pack = pl.pallas_call(
        pack_kernel,
        out_shape=jax.ShapeDtypeStruct((MESH_END, BLOCKS, LANES), f32),
        in_specs=[pl.BlockSpec(memory_space=pltpu.HBM)] * len(parts),
        out_specs=vmem,
        scratch_shapes=[pltpu.VMEM(part.shape, part.dtype) for part in parts[2:]]
        + [pltpu.SemaphoreType.DMA((len(parts),))],
        compiler_params=params,
    )(*[pltpu.with_memory_space_constraint(part, pltpu.HBM) for part in parts])
    first, second = both_sides(pack)
    slice_here = lax.axis_index("tm")
    where = jnp.stack([slice_here // GROUP, slice_here % GROUP, lax.axis_index("space")])
    where = where.astype(jnp.int32)
    small = (
        flux_x,
        flux_y,
        rotation,
        restrict_matrix,
        prolong_matrix.T,
        restrict_index[None, :],
        coarse_inverse,
    )
    stencil_terms, means_matrix, spread_matrix, members, near_inverse = pl.pallas_call(
        prepare_kernel,
        out_shape=(
            jax.ShapeDtypeStruct((ROWS, 240), bf16),
            jax.ShapeDtypeStruct((8, LANES), f32),
            jax.ShapeDtypeStruct((ROWS, 8), f32),
            jax.ShapeDtypeStruct((COARSE_DEV, CELLS_DEV), bf16),
            jax.ShapeDtypeStruct(coarse_inverse.shape, f32),
        ),
        in_specs=[pl.BlockSpec(memory_space=pltpu.HBM)] * len(small),
        out_specs=(vmem,) * 5,
        scratch_shapes=[pltpu.VMEM(part.shape, part.dtype) for part in small[:6]]
        + [pltpu.SemaphoreType.DMA((len(small),))],
        compiler_params=params,
        cost_estimate=pl.CostEstimate(flops=2000000, bytes_accessed=200000, transcendentals=0),
    )(*[pltpu.with_memory_space_constraint(part, pltpu.HBM) for part in small])
    half, places, coefs, start = pl.pallas_call(
        first_phase_kernel,
        out_shape=(
            jax.ShapeDtypeStruct((DOF, BLOCKS, LANES), f32),
            jax.ShapeDtypeStruct((3, 8, TABLE), jnp.int32),
            jax.ShapeDtypeStruct((10, 8, TABLE), f32),
            jax.ShapeDtypeStruct((1, LANES), f32),
        ),
        in_specs=[smem] + [vmem] * 6,
        out_specs=(vmem,) * 4,
        scratch_shapes=march_scratch,
        compiler_params=params,
    )(where, first, pack, second, stencil_terms, members, means_matrix)
    half_first, half_second = both_sides(half)
    late_inverse, half = lax.optimization_barrier((near_inverse, half))
    operator, operator_twice = pl.pallas_call(
        compose_kernel,
        out_shape=tuple(
            jax.ShapeDtypeStruct((2 * reach + 1, 8, 8, LANES), f32)
            for reach in (COARSE_STEPS, 2 * COARSE_STEPS)
        ),
        in_specs=[vmem],
        out_specs=(vmem, vmem),
        compiler_params=params,
        cost_estimate=pl.CostEstimate(flops=12000000, bytes_accessed=900000, transcendentals=0),
    )(late_inverse)
    fine, message = pl.pallas_call(
        second_phase_kernel,
        out_shape=(
            jax.ShapeDtypeStruct((ROWS, CELLS_DEV), f32),
            jax.ShapeDtypeStruct((GROUP * PARTS, 2, LANES), f32),
        ),
        in_specs=[smem] + [vmem] * 9,
        out_specs=(vmem, vmem),
        scratch_shapes=march_scratch,
        compiler_params=params,
    )(
        where, half_first, half, half_second, places, coefs, stencil_terms, members,
        means_matrix, start,
    )

    message, operator, operator_twice, spread_matrix = lax.optimization_barrier(
        (message, operator, operator_twice, spread_matrix)
    )
    axes = ("tm", "space")
    count = GROUP * PARTS
    inside = [[g * count + m for m in range(count)] for g in range(GROUPS)]
    across = [[g * count + m for g in range(GROUPS)] for m in range(count)]
    gathered = lax.all_to_all(message, axes, 0, 0, tiled=True, axis_index_groups=inside)
    ends, own = pl.pallas_call(
        group_kernel,
        out_shape=(
            jax.ShapeDtypeStruct((GROUPS, 8, LANES), f32),
            jax.ShapeDtypeStruct((2, 8, LANES), f32),
        ),
        in_specs=[smem, vmem, vmem],
        out_specs=(vmem, vmem),
        scratch_shapes=[pltpu.VMEM((8 * GROUP, LANES), f32)] * 2,
        compiler_params=params,
    )(where, gathered.reshape(GROUP * PARTS * 2, LANES), operator)
    ends = lax.all_to_all(ends, axes, 0, 0, tiled=True, axis_index_groups=across)
    updated = pl.pallas_call(
        correct_kernel,
        out_shape=jax.ShapeDtypeStruct((DOF, 1, CELLS_DEV), f32),
        in_specs=[smem] + [vmem] * 7,
        out_specs=vmem,
        compiler_params=params,
    )(where, ends, own, operator, operator_twice, fine, members, spread_matrix)
    return updated.transpose(1, 0, 2)


def solution(mesh):
    in_specs = (
        P("tm", None, "space"),
        P(None, "space"),
        P(None, "space"),
        P(None, "space"),
        P(None, "space"),
        P("space"),
        P(),
        P(),
        P(),
        P(),
        P(),
        P("space"),
        P(),
    )
    out_specs = P("tm", None, "space")
    return jax.shard_map(local, mesh=mesh, in_specs=in_specs, out_specs=out_specs, check_vma=False)
```

```python
import functools

import jax
import jax.numpy as jnp
from jax import lax
from jax.experimental import pallas as pl
from jax.experimental.pallas import tpu as pltpu
from jax.sharding import PartitionSpec as P

DOF = 21
CDOF = 4
ROWS = 24
LANES = 128
HALF = 64
CELLS_DEV = 1024
COARSE_DEV = 32
COARSE_STEPS = 4
PARTS = 8
SLICES = 64
GROUP = 8
GROUPS = SLICES // GROUP
BLOCKS = CELLS_DEV // LANES
PHASE_STEPS = 8
WINDOW = 3 * BLOCKS
MESH_END = DOF + 13

coupling = 0.1
opposite = 0.25
highest = lax.Precision.HIGHEST
f32 = jnp.float32
bf16 = jnp.bfloat16
vmem = pl.BlockSpec(memory_space=pltpu.VMEM)


def lane_gather(values, index):
    numbers = lax.GatherDimensionNumbers(
        offset_dims=(),
        collapsed_slice_dims=(1,),
        start_index_map=(1,),
        operand_batching_dims=(0,),
        start_indices_batching_dims=(0,),
    )
    return lax.gather(
        values, index[..., None], numbers, (1, 1), mode=lax.GatherScatterMode.PROMISE_IN_BOUNDS
    )


def two_terms(values):
    high = values.astype(bf16)
    return high, (values - high.astype(f32)).astype(bf16)


def lanes_of(block, count=1):
    return slice(block * LANES, (block + count) * LANES)


def in_order(odd, refs, place):
    one, two = refs[0][place], refs[2][place]
    return jnp.where(odd, one, two), refs[1][place], jnp.where(odd, two, one)


def fill_field(odd, state_refs, field):
    edge = jnp.zeros((ROWS, LANES), f32)
    field[:, lanes_of(0)] = edge
    field[:, lanes_of(WINDOW + 1)] = edge
    rest = jnp.zeros((ROWS - DOF, LANES), f32)
    for b in range(BLOCKS):
        whole = in_order(odd, state_refs, (slice(0, 16), b, slice(None)))
        tail = in_order(odd, state_refs, (slice(16, DOF), b, slice(None)))
        for part in range(3):
            here = lanes_of(1 + part * BLOCKS + b)
            field[0:16, here] = whole[part]
            field[16:ROWS, here] = jnp.concatenate([tail[part], rest], axis=0)


def fill_tables(odd, mesh_refs, places, coefs):
    lane = lax.broadcasted_iota(jnp.int32, (BLOCKS, LANES), 1)

    def spread(table, row, part, tile):
        for b in range(BLOCKS):
            here = lanes_of(1 + part * BLOCKS + b)
            table[row, :, here] = jnp.broadcast_to(tile[b : b + 1, :], (8, LANES))

    for row in range(MESH_END - DOF):
        for part, tile in enumerate(in_order(odd, mesh_refs, DOF + row)):
            if row < 3:
                target = tile.astype(jnp.int32) + lane
                within = (target >= 0) & (target < LANES)
                spread(
                    places, row, part, (target & (LANES - 1)) + jnp.where(within, 0, LANES)
                )
            else:
                spread(coefs, row - 3, part, tile)


def block_rate(source, block, places, coefs, stencil, low_half):
    here = lanes_of(block)
    centre = []
    around = []
    for r in range(3):
        rows = slice(8 * r, 8 * r + 8)
        centre.append(source[rows, here])
        around.append(
            jnp.where(low_half, source[rows, lanes_of(block + 1)], source[rows, lanes_of(block - 1)])
        )
    sums = [[None] * 3 for _ in range(3)]
    for e in range(3):
        place = places[e, :, here]
        index = place & (LANES - 1)
        within = place < LANES
        found = [lane_gather(piece, index) for piece in centre + around]
        for r in range(3):
            difference = jnp.where(within, found[r], found[3 + r]) - centre[r]
            for a in range(3):
                term = coefs[3 * a + e, :, here] * difference
                sums[a][r] = term if e == 0 else sums[a][r] + term
    turned = [coefs[9, :, here] * piece for piece in centre]
    stacked = jnp.concatenate(sums[0] + sums[1] + turned + [jnp.zeros((8, LANES), f32)], axis=0)
    high, low = two_terms(stacked)
    mixed = jnp.dot(
        stencil, jnp.concatenate([high, low, high], axis=0), preferred_element_type=f32
    )
    return mixed + jnp.concatenate(sums[2], axis=0)


def march(field, middle, places, coefs, stencil_ref):
    low_half = lax.broadcasted_iota(jnp.int32, (8, LANES), 1) < HALF
    edge = jnp.zeros((ROWS, LANES), f32)
    middle[:, lanes_of(0)] = edge
    middle[:, lanes_of(WINDOW + 1)] = edge

    stencil = stencil_ref[...]
    for index in range(PHASE_STEPS):
        for b in range(1 + index, 1 + WINDOW - index):
            rate = block_rate(field, b, places, coefs, stencil, low_half)
            middle[:, lanes_of(b)] = field[:, lanes_of(b)] + rate
        for b in range(2 + index, WINDOW - index):
            rate = block_rate(middle, b, places, coefs, stencil, low_half)
            here = lanes_of(b)
            field[:, here] = 0.5 * (field[:, here] + middle[:, here] + rate)


def pack_kernel(states, coriolis, neighbour, edge_x, edge_y, edge_damp, out, *scratch):
    buffers, done = scratch[:4], scratch[4]
    last = MESH_END - 1
    pairs = [(states, out.at[0:DOF]), (coriolis, out.at[last : last + 1])]
    pairs += list(zip((neighbour, edge_x, edge_y, edge_damp), buffers))
    copies = [
        pltpu.make_async_copy(source, target, done.at[i])
        for i, (source, target) in enumerate(pairs)
    ]
    for copy in copies:
        copy.start()
    for copy in copies:
        copy.wait()
    for i, buffer in enumerate(buffers):
        rows = buffer[...].astype(f32)
        for e in range(3):
            for b in range(BLOCKS):
                out[DOF + 3 * i + e, b : b + 1, :] = rows[e : e + 1, lanes_of(b)]


def added(terms):
    while len(terms) > 1:
        terms = [sum(terms[i : i + 2][1:], terms[i]) for i in range(0, len(terms), 2)]
    return terms[0]


def restricted(values, members, restrict_matrix):
    contract = (((1,), (1,)), ((), ()))
    totals = jnp.zeros((ROWS, COARSE_DEV), f32)
    for term in two_terms(values):
        totals = totals + lax.dot_general(term, members, contract, preferred_element_type=f32)
    counts = lax.dot_general(
        jnp.ones((16, CELLS_DEV), bf16), members, contract, preferred_element_type=f32
    )[0:1]
    result = added(
        [restrict_matrix[0:CDOF, d : d + 1] * totals[d : d + 1, :] for d in range(DOF)]
    )
    result = result / counts
    return jnp.concatenate([result[i : i + 1, :] for i in range(CDOF)], axis=1)


def flipped(tiles, even_row):
    up = pltpu.roll(jnp.concatenate([tiles[1:], tiles[:1]], axis=0), 7, axis=1)
    down = pltpu.roll(jnp.concatenate([tiles[7:], tiles[:7]], axis=0), 1, axis=1)
    return jnp.where(even_row, up, down)


def composed(reach, inverse_ref, first, last):
    shape = (8, 8, LANES)
    row = lax.broadcasted_iota(jnp.int32, shape, 1)
    lane = lax.broadcasted_iota(jnp.int32, shape, 2)
    even_row = row % 2 == 0
    first_lane = lane == 0
    last_lane = lane == LANES - 1
    own = 1.0 - 2.0 * coupling - opposite
    blocks = []
    for by in range(CDOF):
        pieces = []
        for i in range(CDOF):
            j = (i - by) % CDOF
            for h in range(2):
                pieces.append(inverse_ref[i, j : j + 1, lanes_of(h)])
        blocks.append(jnp.concatenate(pieces, axis=0)[None])
    for repeat in range(first, last):
        swapped = {o: flipped(tiles, even_row) for o, tiles in reach.items()}
        blended = {}
        for o in range(-repeat - 1, repeat + 2):
            total = jnp.zeros(shape, f32)
            if o in reach:
                total = own * reach[o] + opposite * swapped[o]
            if o - 1 in reach:
                edge = jnp.where(last_lane, swapped[o - 1], reach[o - 1])
                total = total + coupling * pltpu.roll(edge, 1, axis=2)
            if o + 1 in reach:
                edge = jnp.where(first_lane, swapped[o + 1], reach[o + 1])
                total = total + coupling * pltpu.roll(edge, LANES - 1, axis=2)
            blended[o] = total
        reach = {}
        for o, tiles in blended.items():
            total = blocks[0] * tiles
            for by in range(1, CDOF):
                turned = jnp.concatenate([tiles[8 - 2 * by :], tiles[: 8 - 2 * by]], axis=0)
                total = total + blocks[by] * pltpu.roll(turned, 2 * by, axis=1)
            reach[o] = total
    return reach


def keep_operator(out, reach):
    size = max(reach)
    for o, tiles in reach.items():
        out[o + size] = tiles if o == 0 else pltpu.roll(tiles, -o % LANES, axis=2)


def prepare_kernel(*refs):
    sources, outs, buffers, done = refs[:7], refs[7:14], refs[14:20], refs[20]
    stencil_out, means_out, spread_out, members_out, operator_out, once_out, inverse_out = outs
    copies = [
        pltpu.make_async_copy(source, buffer, done.at[i])
        for i, (source, buffer) in enumerate(zip(sources, buffers + (inverse_out,)))
    ]
    for copy in copies:
        copy.start()
    for copy in copies:
        copy.wait()
    flux_x, flux_y, rotation, means, spread, index = [buffer[...] for buffer in buffers]
    side = ROWS - DOF
    wide = [jnp.pad(m, ((0, side), (0, side))) for m in (flux_x, flux_y, rotation)]
    stencil = jnp.concatenate(wide + [jnp.zeros((ROWS, 8), f32)], axis=1)
    high = stencil.astype(bf16).astype(f32)
    stencil_out[...] = jnp.concatenate([high, high, stencil - high], axis=1).astype(bf16)
    means_out[...] = jnp.pad(means, ((0, 8 - CDOF), (0, LANES - DOF)))
    turned = jnp.pad(spread, ((0, 8 - CDOF), (0, LANES - DOF))).T
    spread_out[...] = turned[0:ROWS, :]
    members = lax.broadcasted_iota(jnp.int32, (COARSE_DEV, CELLS_DEV), 0) == index
    members_out[...] = members.astype(f32).astype(bf16)
    turn = lax.broadcasted_iota(jnp.int32, (8, 8, LANES), 0)
    reach = composed({0: jnp.where(turn == 0, 1.0, 0.0)}, inverse_out, 0, COARSE_STEPS)
    keep_operator(operator_out, reach)
    for o, tiles in reach.items():
        once_out[o + COARSE_STEPS] = tiles


def first_phase_kernel(
    where_ref, first, centre, second, stencil_ref, members_ref, matrix_ref,
    out, places, coefs, start_out, field, middle,
):
    odd = where_ref[2] % 2 == 1
    packs = (first, centre, second)
    fill_tables(odd, packs, places, coefs)
    fill_field(odd, packs, field)
    start = field[:, lanes_of(1 + BLOCKS, BLOCKS)]
    start_out[...] = restricted(start, members_ref[...], matrix_ref[...])
    march(field, middle, places, coefs, stencil_ref)
    for b in range(BLOCKS):
        out[:, b, :] = field[0:DOF, lanes_of(1 + BLOCKS + b)]


def second_phase_kernel(
    where_ref, first, centre, second, places, coefs, stencil_ref, members_ref, matrix_ref, start_ref,
    out, message, field, middle,
):
    fill_field(where_ref[2] % 2 == 1, (first, centre, second), field)
    march(field, middle, places, coefs, stencil_ref)
    fine = field[:, lanes_of(1 + BLOCKS, BLOCKS)]
    out[...] = fine
    rows = jnp.concatenate(
        [restricted(fine, members_ref[...], matrix_ref[...]), start_ref[...]], axis=0
    )
    for copy in range(GROUP * PARTS):
        message[copy] = rows


def compose_kernel(once_ref, inverse_ref, out):
    size = COARSE_STEPS
    reach = {o: once_ref[o + size] for o in range(-size, size + 1)}
    keep_operator(out, composed(reach, inverse_ref, size, 2 * size))


def coarse_slice(vector, operator_ref):
    turns = [vector] + [pltpu.roll(vector, d, axis=0) for d in range(1, 8)]
    reach = operator_ref.shape[0] // 2
    shares = []
    for o in range(-reach, reach + 1):
        share = added([operator_ref[o + reach, d] * turns[d] for d in range(8)])
        shares.append(share if o == 0 else pltpu.roll(share, o % LANES, axis=1))
    return added(shares)


def group_kernel(where_ref, gathered, operator_ref, ends_out, own_out, finish, start):
    group = where_ref[0]
    place = where_ref[1]
    quarter = lax.broadcasted_iota(jnp.int32, (GROUP, LANES), 1) // COARSE_DEV
    for kind, ref in enumerate((finish, start)):
        for i in range(CDOF):
            for h in range(2):
                held = jnp.zeros((GROUP, LANES), f32)
                for q in range(4):
                    p = 4 * h + q
                    rows = gathered[pl.ds(2 * p + kind, GROUP, stride=2 * PARTS), :]
                    by = (q - i) * COARSE_DEV % LANES
                    moved = rows if by == 0 else pltpu.roll(rows, by, axis=1)
                    held = jnp.where(quarter == q, moved, held)
                ref[pl.ds((2 * i + h) * GROUP, GROUP), :] = held

    def of_slice(ref, n):
        return ref[pl.ds(n, 8, stride=GROUP), :]

    chain = None
    own = jnp.zeros((8, LANES), f32)
    for n in range(GROUP):
        coarse = coarse_slice(of_slice(start, n), operator_ref)
        if n == 0:
            coarse = jnp.where(group > 0, coarse, 0.0)
        jump = of_slice(finish, n) - coarse
        chain = jump if n == 0 else coarse_slice(chain, operator_ref) + jump
        own = jnp.where(place == n, chain, own)
    for copy in range(GROUPS):
        ends_out[copy] = chain
    own_out[0] = own
    own_out[1] = finish[pl.ds(place, 8, stride=GROUP), :]


def correct_kernel(
    where_ref, ends, own_ref, operator_ref, twice_ref, fine_ref, members_ref, matrix_ref, out
):
    group = where_ref[0]
    place = where_ref[1]
    part = where_ref[2]

    def advance(count, vector, ref):
        return lax.fori_loop(0, count, lambda n, now: coarse_slice(now, ref), vector)

    def link(k, vector):
        return advance(GROUP // 2, vector, twice_ref) + ends[k]

    before = lax.fori_loop(1, group, link, ends[0])
    count = jnp.where(group > 0, place + 1, 0)
    before = advance(count % 2, advance(count // 2, before, twice_ref), operator_ref)
    chain = own_ref[0] + jnp.where(group > 0, before, 0.0)
    change = chain - own_ref[1]
    upper = part >= PARTS // 2
    spread = jnp.zeros((ROWS, LANES), f32)
    for i in range(CDOF):
        chosen = jnp.where(upper, change[2 * i + 1 : 2 * i + 2], change[2 * i : 2 * i + 1])
        spread = spread + matrix_ref[:, i : i + 1] * jnp.broadcast_to(chosen, (ROWS, LANES))
    spread = pltpu.roll(spread, (4 - part % 4) * COARSE_DEV % LANES, axis=1)[:, 0:COARSE_DEV]
    total = fine_ref[...]
    for term in two_terms(spread):
        total = total + jnp.dot(term, members_ref[...], preferred_element_type=f32)
    for d in range(DOF):
        out[d] = total[d : d + 1, :]


TABLE = (WINDOW + 2) * LANES
march_scratch = [pltpu.VMEM((ROWS, TABLE), f32)] * 2


params = pltpu.CompilerParams(vmem_limit_bytes=32 * 1024 * 1024)


def both_sides(values):
    pairs = [(i, i ^ 1) for i in range(PARTS)]
    others = [(i, (((i + 1) ^ 1) - 1) % PARTS) for i in range(PARTS)]
    return lax.ppermute(values, "space", pairs), lax.ppermute(values, "space", others)


smem = pl.BlockSpec(memory_space=pltpu.SMEM)


def local(
    states,
    neighbour,
    edge_x,
    edge_y,
    edge_damp,
    coriolis,
    flux_x,
    flux_y,
    rotation,
    restrict_matrix,
    prolong_matrix,
    restrict_index,
    coarse_inverse,
):
    parts = (
        states.transpose(1, 0, 2).reshape(DOF, BLOCKS, LANES),
        coriolis.reshape(1, BLOCKS, LANES),
        neighbour,
        edge_x,
        edge_y,
        edge_damp,
    )
    pack = pl.pallas_call(
        pack_kernel,
        out_shape=jax.ShapeDtypeStruct((MESH_END, BLOCKS, LANES), f32),
        in_specs=[pl.BlockSpec(memory_space=pltpu.HBM)] * len(parts),
        out_specs=vmem,
        scratch_shapes=[pltpu.VMEM(part.shape, part.dtype) for part in parts[2:]]
        + [pltpu.SemaphoreType.DMA((len(parts),))],
        compiler_params=params,
    )(*[pltpu.with_memory_space_constraint(part, pltpu.HBM) for part in parts])
    first, second = both_sides(pack)
    slice_here = lax.axis_index("tm")
    where = jnp.stack([slice_here // GROUP, slice_here % GROUP, lax.axis_index("space")])
    where = where.astype(jnp.int32)
    small = (
        flux_x,
        flux_y,
        rotation,
        restrict_matrix,
        prolong_matrix.T,
        restrict_index[None, :],
        coarse_inverse,
    )
    once = jax.ShapeDtypeStruct((2 * COARSE_STEPS + 1, 8, 8, LANES), f32)
    (
        stencil_terms, means_matrix, spread_matrix, members, operator, reach, near_inverse
    ) = pl.pallas_call(
        prepare_kernel,
        out_shape=(
            jax.ShapeDtypeStruct((ROWS, 240), bf16),
            jax.ShapeDtypeStruct((8, LANES), f32),
            jax.ShapeDtypeStruct((ROWS, 8), f32),
            jax.ShapeDtypeStruct((COARSE_DEV, CELLS_DEV), bf16),
            once,
            once,
            jax.ShapeDtypeStruct(coarse_inverse.shape, f32),
        ),
        in_specs=[pl.BlockSpec(memory_space=pltpu.HBM)] * len(small),
        out_specs=(vmem,) * 7,
        scratch_shapes=[pltpu.VMEM(part.shape, part.dtype) for part in small[:6]]
        + [pltpu.SemaphoreType.DMA((len(small),))],
        compiler_params=params,
        cost_estimate=pl.CostEstimate(flops=2000000, bytes_accessed=200000, transcendentals=0),
    )(*[pltpu.with_memory_space_constraint(part, pltpu.HBM) for part in small])
    half, places, coefs, start = pl.pallas_call(
        first_phase_kernel,
        out_shape=(
            jax.ShapeDtypeStruct((DOF, BLOCKS, LANES), f32),
            jax.ShapeDtypeStruct((3, 8, TABLE), jnp.int32),
            jax.ShapeDtypeStruct((10, 8, TABLE), f32),
            jax.ShapeDtypeStruct((1, LANES), f32),
        ),
        in_specs=[smem] + [vmem] * 6,
        out_specs=(vmem,) * 4,
        scratch_shapes=march_scratch,
        compiler_params=params,
    )(where, first, pack, second, stencil_terms, members, means_matrix)
    half_first, half_second = both_sides(half)
    reach, late_inverse, half = lax.optimization_barrier((reach, near_inverse, half))
    operator_twice = pl.pallas_call(
        compose_kernel,
        out_shape=jax.ShapeDtypeStruct((4 * COARSE_STEPS + 1, 8, 8, LANES), f32),
        in_specs=[vmem] * 2,
        out_specs=vmem,
        compiler_params=params,
        cost_estimate=pl.CostEstimate(flops=9000000, bytes_accessed=900000, transcendentals=0),
    )(reach, late_inverse)
    fine, message = pl.pallas_call(
        second_phase_kernel,
        out_shape=(
            jax.ShapeDtypeStruct((ROWS, CELLS_DEV), f32),
            jax.ShapeDtypeStruct((GROUP * PARTS, 2, LANES), f32),
        ),
        in_specs=[smem] + [vmem] * 9,
        out_specs=(vmem, vmem),
        scratch_shapes=march_scratch,
        compiler_params=params,
    )(
        where, half_first, half, half_second, places, coefs, stencil_terms, members,
        means_matrix, start,
    )

    message, operator, operator_twice, spread_matrix = lax.optimization_barrier(
        (message, operator, operator_twice, spread_matrix)
    )
    axes = ("tm", "space")
    count = GROUP * PARTS
    inside = [[g * count + m for m in range(count)] for g in range(GROUPS)]
    across = [[g * count + m for g in range(GROUPS)] for m in range(count)]
    gathered = lax.all_to_all(message, axes, 0, 0, tiled=True, axis_index_groups=inside)
    ends, own = pl.pallas_call(
        group_kernel,
        out_shape=(
            jax.ShapeDtypeStruct((GROUPS, 8, LANES), f32),
            jax.ShapeDtypeStruct((2, 8, LANES), f32),
        ),
        in_specs=[smem, vmem, vmem],
        out_specs=(vmem, vmem),
        scratch_shapes=[pltpu.VMEM((8 * GROUP, LANES), f32)] * 2,
        compiler_params=params,
    )(where, gathered.reshape(GROUP * PARTS * 2, LANES), operator)
    ends = lax.all_to_all(ends, axes, 0, 0, tiled=True, axis_index_groups=across)
    updated = pl.pallas_call(
        correct_kernel,
        out_shape=jax.ShapeDtypeStruct((DOF, 1, CELLS_DEV), f32),
        in_specs=[smem] + [vmem] * 7,
        out_specs=vmem,
        compiler_params=params,
    )(where, ends, own, operator, operator_twice, fine, members, spread_matrix)
    return updated.transpose(1, 0, 2)


def solution(mesh):
    in_specs = (
        P("tm", None, "space"),
        P(None, "space"),
        P(None, "space"),
        P(None, "space"),
        P(None, "space"),
        P("space"),
        P(),
        P(),
        P(),
        P(),
        P(),
        P("space"),
        P(),
    )
    out_specs = P("tm", None, "space")
    return jax.shard_map(local, mesh=mesh, in_specs=in_specs, out_specs=out_specs, check_vma=False)
```
